512 devices in a mesh: seq: 64 (over x, z_hi, y), tp: 8 (over z_lo, core).
Axes of the slice: x: 4, y: 4, z: 16 (z_hi: 4, z_lo: 4; z = z_hi * 4 + z_lo), core: 2. Of those that a mesh axis runs over, the one named last changes fastest.
Arguments:
- signal: bfloat16 [8192, 4096], P('seq', 'tp'), may hold values from -6 to 6
- gate_input: bfloat16 [8192, 4096], P('seq', 'tp'), may hold values from -6 to 6
- filters: bfloat16 [1024, 4096], P(None, 'tp'), may hold values from -0.1875 to 0.1875
- skip_weight: float32 [4096], P('tp'), may hold values from 0.2 to 5, as said below
- doc_lengths: int32 [16], replicated, may hold values from 1 to 8, 64 in all
- grad_out: bfloat16 [8192, 4096], P('seq', 'tp'), may hold values from -6 to 6
Outputs:
- output: bfloat16 [8192, 4096], P('seq', 'tp')
- grad_signal: bfloat16 [8192, 4096], P('seq', 'tp')
- grad_gate: bfloat16 [8192, 4096], P('seq', 'tp')
- grad_filters: float32 [1024, 4096], P('seq', 'tp')
The draws below stay inside these ranges and needn't reach their ends.
Inputs may be any that keep to these rules, and one draw needn't show every extreme that they name: `doc_lengths`: lengths of the 16 packed documents in blocks of 128 tokens; they sum to 64 and the largest is exactly 8. `skip_weight`: positive per-channel weights.
All inputs are finite; a program needn't handle non-finite values.
Results may differ from the reference program's by a relative error of at most 0.0049.
Values may be sent and summed in bfloat16 or wider, within the bound.
A program may use at most 64 MiB of HBM per device.

```python
import math
import jax
import jax.numpy as jnp
import numpy as np
from jax import lax

D = 4096
TOK_DEV = 128
MOSTDOC = 8
TOKENS = 8192
DOCS = 16
LMAX = 1024
N_SEQ = 64


def draw_skip_weight(key, part):
    key = jax.random.fold_in(key, 7)
    channel_pos = jnp.arange(D, dtype=jnp.float32) / D
    ramp_values = 0.5 + 1.5 * channel_pos
    spread_values = jax.random.uniform(key, (D,), jnp.float32, 0.7, 1.3)
    return ramp_values * spread_values


def block_levels(stream_key, dims, cuts, low, largest):
    level = 1.0
    for position, parts in cuts:
        steps = jax.random.uniform(jax.random.fold_in(jax.random.fold_in(stream_key, 6), position), (parts,), jnp.float32, low / len(cuts), largest / len(cuts))
        level = level * jnp.repeat(jnp.exp(steps), dims[position] // parts).reshape((-1,) + (1,) * (len(dims) - 1 - position))
    return level


def profile(number_of, total, most, slope):
    weights = [(1 << 20) // math.isqrt(rank ** slope) + 1 for rank in range(2, number_of + 1)]
    surplus, counts = total - most - (number_of - 1), [1] * (number_of - 1)
    while surplus > 0:
        movable = [i for i in range(number_of - 1) if counts[i] < most]
        mass, left = sum([weights[i] for i in movable]), surplus
        for i in movable:
            extra = min(most - counts[i], max(1, left * weights[i] // mass), surplus)
            counts[i] = counts[i] + extra
            surplus = surplus - extra
    return np.array([most] + counts)


def ragged(key, number_of, total, reach, lean):
    if number_of == 2:
        one = jax.random.randint(key, (), max(1, total - reach), min(reach, total - 1) + 1)
        return jnp.stack([one, total - one])
    tallies = jnp.asarray(profile(number_of, total, reach, lean), jnp.int32)
    couples = (number_of - 1) // 2
    giver, sink = tallies[1:1 + 2 * couples:2], tallies[2:2 + 2 * couples:2]
    slack = jnp.minimum(giver - 1, reach - sink)
    moved = jax.random.randint(jax.random.fold_in(key, 1), (couples,), 0, 1 << 20) % (slack + 1)
    tallies = tallies.at[1:1 + 2 * couples:2].set(giver - moved).at[2:2 + 2 * couples:2].set(sink + moved)
    return tallies[jax.random.permutation(jax.random.fold_in(key, 2), number_of)]


def bell_draw(stream_key, dims, width, bound, cuts=(), kind=jnp.bfloat16):
    values = jax.random.normal(stream_key, dims, jnp.float32) * width
    if len(cuts) > 0:
        values = block_levels(stream_key, dims, cuts, -0.22, 0.18) * values
    return jnp.clip(values, min=-bound, max=bound).astype(kind)


def setup_inputs(seed: int = 0) -> dict:
    key_list = jax.random.split(jax.random.key(seed), 7)
    signal = bell_draw(key_list[0], (TOKENS, D), 1.0, 6.0, ((0, 64), (1, 8)))
    gate_input = bell_draw(key_list[1], (TOKENS, D), 1.0, 6.0, ((0, 64), (1, 8)))
    filters = bell_draw(key_list[2], (LMAX, D), LMAX ** -0.5, 0.1875, ((1, 8),))
    skip_weight = draw_skip_weight(jax.random.fold_in(key_list[6], 71), 0)
    doc_lengths = ragged(key_list[4], DOCS, N_SEQ, MOSTDOC, 0).astype(jnp.int32)
    grad_out = bell_draw(key_list[5], (TOKENS, D), 1.0, 6.0, ((0, 64), (1, 8)))
    return {"signal": signal, "gate_input": gate_input, "filters": filters, "skip_weight": skip_weight, "doc_lengths": doc_lengths, "grad_out": grad_out}


EPSILON = 1e-06

def block_starts(doc_lengths, amount):
    finish = jnp.cumsum(doc_lengths).astype(jnp.int32)
    anchor = (finish - doc_lengths).astype(jnp.int32)
    numbers = jnp.arange(amount, dtype=jnp.int32)[:, None]
    inside = (anchor[None, :] <= numbers) & (numbers < finish[None, :])
    return lax.optimization_barrier(jnp.sum(jnp.where(inside, anchor[None, :], 0), axis=1)).astype(jnp.int32)

def causal_conv(values, taps, starts):
    amount = values.shape[0] // TOK_DEV
    pieces = values.reshape(amount, TOK_DEV, -1)
    signal_spec = jnp.fft.rfft(pieces, n=2 * TOK_DEV, axis=1)
    tap_blocks = taps.reshape(MOSTDOC, TOK_DEV, -1)
    previous = jnp.concatenate([jnp.zeros_like(tap_blocks[:1]), tap_blocks[:-1]], axis=0)
    kernel_spec = jnp.fft.rfft(jnp.concatenate([previous, tap_blocks], axis=1), axis=1)
    numbers = jnp.arange(amount, dtype=jnp.int32)
    accum = jnp.zeros(signal_spec.shape, signal_spec.dtype)
    for distance in range(MOSTDOC):
        usable = numbers - distance >= starts
        shifted = jnp.roll(signal_spec, distance, axis=0)
        accum = accum + jnp.where(usable[:, None, None], kernel_spec[distance][None] * shifted, 0.0)
    result = jnp.fft.irfft(accum, n=2 * TOK_DEV, axis=1)[:, TOK_DEV:, :]
    return result.reshape(values.shape)

def reference(signal, gate_input, filters, skip_weight, doc_lengths, grad_out):
    starts = block_starts(doc_lengths, signal.shape[0] // TOK_DEV)
    signal_f = signal.astype(jnp.float32)
    taps_f = filters.astype(jnp.float32)
    convolved, pullback = jax.vjp(lambda first_arg, second_arg: causal_conv(first_arg, second_arg, starts), signal_f, taps_f)
    mixed = convolved + skip_weight[None, :] * signal_f
    gate_f = gate_input.astype(jnp.float32)
    gated = gate_f * mixed
    inverse_rms = lax.rsqrt(lax.optimization_barrier(jnp.mean(gated * gated, axis=1, keepdims=True)) + EPSILON)
    output = (gated * inverse_rms).astype(jnp.bfloat16)
    cotangent = grad_out.astype(jnp.float32)
    projection = lax.optimization_barrier(jnp.mean(cotangent * gated, axis=1, keepdims=True))
    grad_gated = cotangent * inverse_rms - gated * (projection * inverse_rms * inverse_rms * inverse_rms)
    grad_gate = (grad_gated * mixed).astype(jnp.bfloat16)
    grad_mixed = lax.optimization_barrier((grad_gated * gate_f).astype(jnp.bfloat16)).astype(jnp.float32)
    grad_sig, grad_taps = pullback(grad_mixed)
    grad_signal = (grad_sig + skip_weight[None, :] * grad_mixed).astype(jnp.bfloat16)
    grad_filters = grad_taps * TOKENS ** (-0.5)
    return (output, grad_signal, grad_gate, grad_filters)
```

```python
import functools
import math

import jax
import jax.numpy as jnp
import numpy as np
from jax import lax
from jax.experimental import pallas as pl
from jax.experimental.pallas import tpu as pltpu
from jax.sharding import PartitionSpec as P

EPSILON = 1e-06
MESH = pl.DeviceIdType.MESH
T = 128
C = 128
Q = 4
LAGS = 8
REL = 20
F32 = jnp.float32
BF16 = jnp.bfloat16


def tables():
    freq = np.arange(T)[:, None]
    time = np.arange(2 * T)[None, :]
    phase = (freq * time % (2 * T)) * (2.0 * math.pi / (2 * T))
    real, imag = np.cos(phase), -np.sin(phase)
    imag[0] = 1 - 2 * (np.arange(2 * T) % 2)
    forward = np.concatenate([real, imag], axis=0)
    scale = np.full((2 * T, 1), 1.0 / T)
    scale[0] = scale[T] = 0.5 / T
    backward = (forward * scale).T

    def split(table):
        table = table.astype(np.float32)
        high = table.astype(jnp.bfloat16)
        low = (table - high.astype(np.float32)).astype(jnp.bfloat16)
        return high, low

    high, low = split(forward)
    first = np.concatenate([high[:, :T], low[:, :T]], axis=1)
    second = np.concatenate([high[:, T:], low[:, T:]], axis=1)
    back_high, back_low = split(backward)
    return np.stack([first, second, back_high, back_low])


def dot(a, b):
    return jnp.dot(a, b, preferred_element_type=F32)


def kernel(
    docs, skip, signal, gate, filters, cotangent, table,
    out, gsig, ggate, gfilt,
    sig_v, gate_v, cot_v, taps, tab, xbuf, dbuf, spec, dspec, kr, ki, kn, prod, gprod,
    conv_s, conv_r, back_s, back_r, zval, dz, tpbuf, gf_s, gf_r, gx_s, gx_r, gz_s, gz_r,
    load_sem, za_s, za_r, yf_s, yf_r, xh_s, xh_r, zb_s, zb_r, tp_s, tp_r,
    da_s, da_r, df_s, df_r, dh_s, dh_r, db_s, db_r, gy_ss, gy_rs, gx_ss, gx_rs, gz_ss, gz_rs,
):
    seq, tpi = lax.axis_index("seq"), lax.axis_index("tp")
    x, z, y = seq // 16, (seq // 4) % 4, seq % 4

    def at(xx, zz, yy):
        return (lax.rem(xx, Q) * 16 + lax.rem(zz, Q) * 4 + lax.rem(yy, Q), tpi)

    def send(src, dst, ssem, rsem, target):
        return pltpu.make_async_remote_copy(
            src_ref=src, dst_ref=dst, send_sem=ssem, recv_sem=rsem, device_id=target, device_id_type=MESH
        )

    barrier = pltpu.get_barrier_semaphore()
    partners = [at(x, z + k, y) for k in (2, 1, 3)] + [at(x, z, y + k) for k in (1, 2, 3)]
    partners += [at(x + i, z, y + k) for i in (1, 3) for k in range(Q)] + [at(x + 2, z, y)]
    partners += [(seq, lax.rem(tpi + k, 8)) for k in range(1, 8)]
    for partner in partners:
        pl.semaphore_signal(barrier, inc=1, device_id=partner, device_id_type=MESH)

    lanes = pl.ds(pl.multiple_of(z * C, C), C)
    loads = [
        pltpu.make_async_copy(table, tab, load_sem.at[0]),
        pltpu.make_async_copy(filters.at[:, lanes], taps, load_sem.at[1]),
        pltpu.make_async_copy(signal, sig_v, load_sem.at[2]),
        pltpu.make_async_copy(gate, gate_v, load_sem.at[3]),
        pltpu.make_async_copy(cotangent, cot_v, load_sem.at[4]),
    ]
    for load in loads:
        load.start()

    early, late = [], []
    for zp in range(Q):
        block = 16 * x + 4 * zp + y
        begin, first, last = jnp.int32(0), jnp.int32(0), jnp.int32(0)
        for k in range(docs.shape[0]):
            end = begin + docs[k]
            inside = (begin <= block) & (block < end)
            first = jnp.where(inside, begin, first)
            last = jnp.where(inside, end, last)
            begin = end
        early.append([jnp.where(block - d >= first, 1.0, 0.0).astype(F32) for d in range(LAGS)])
        late.append([jnp.where(block + d < last, 1.0, 0.0).astype(F32) for d in range(LAGS)])

    row0 = lax.broadcasted_iota(jnp.int32, (T, C), 0) == 0
    loads[0].wait()
    loads[1].wait()
    for d in range(LAGS):
        tap = taps[d * T : (d + 1) * T, :]
        value = dot(tab[1], jnp.concatenate([tap, tap], axis=0))
        if d > 0:
            before = taps[(d - 1) * T : d * T, :]
            value += dot(tab[0], jnp.concatenate([before, before], axis=0))
        real, imag = value[:T], value[T:]
        kr[d] = real
        ki[d] = jnp.where(row0, 0.0, imag)
        kn[d] = jnp.where(row0, imag, real)
    for load in loads[2:]:
        load.wait()
    pl.semaphore_wait(barrier, len(partners))

    def chunk(k):
        return pl.ds(pl.multiple_of(lax.rem(k, Q) * C, C), C)

    def spread(source, buf, shift, xstep, za_s, za_r, yf_s, yf_r, xh_s, xh_r):
        waits = []
        own = shift + 4 * z + y
        for k in (2, 1, 3):
            copy = send(source.at[:, chunk(z + k)], buf.at[own], za_s.at[k - 1], za_r.at[k - 1], at(x, z + k, y))
            copy.start()
            waits.append(copy)
        buf[own] = source[:, lanes]
        forward = xstep == 1
        halo_shift = 0 if forward else 16
        sent = []
        for k in (0, 1, 3, 2):
            zsrc = lax.rem(z + 4 - k, Q)
            if k:
                send(source.at[:, lanes], buf.at[shift + 4 * zsrc + y], za_s.at[k - 1], za_r.at[k - 1], at(x, z, y)).wait_recv()
            slot = buf.at[shift + 4 * zsrc + y]
            far, near = (zsrc == 3, zsrc == 2) if forward else (zsrc == 0, zsrc == 1)
            for j in (2, 1, 3, 0):
                yp = lax.rem(y + j, Q)
                ahead = yp > y if forward else yp < y
                if j:
                    needed = jnp.logical_not(far) | ahead
                    copy = send(slot, slot, yf_s.at[k, j - 1], yf_r.at[zsrc, j - 1], at(x, z, yp))
                    pl.when(needed)(copy.start)
                    sent.append((needed, copy))
                behind = yp < y if forward else yp > y
                needed = far | (near & behind)
                side = jnp.where(far, 1, 0)
                hslot = buf.at[halo_shift + lax.rem(4 * zsrc + 8, 16) % 8 + y]
                copy = send(slot, hslot, xh_s.at[k, j], xh_r.at[side, j], at(x + xstep, z, yp))
                pl.when(needed)(copy.start)
                sent.append((needed, copy))
        for zsrc in range(Q):
            for j in (1, 2, 3):
                ysrc = lax.rem(y + 4 - j, Q)
                slot = buf.at[shift + 4 * zsrc + ysrc]
                copy = send(slot, slot, yf_s.at[0, j - 1], yf_r.at[zsrc, j - 1], at(x, z, ysrc))
                if zsrc == (3 if forward else 0):
                    pl.when(y > ysrc if forward else y < ysrc)(copy.wait_recv)
                else:
                    copy.wait_recv()
        for side in (0, 1):
            for j in range(Q):
                ysrc = lax.rem(y + 4 - j, Q)
                quad = (2 + side) if forward else (1 - side)
                slot = buf.at[halo_shift + (4 * quad) % 8 + ysrc]
                copy = send(slot, slot, xh_s.at[0, j], xh_r.at[side, j], at(x + 4 - xstep, z, ysrc))
                if side:
                    copy.wait_recv()
                else:
                    pl.when(y < ysrc if forward else y > ysrc)(copy.wait_recv)
        return waits, sent

    def transform(tbl, buf, start, count, result):
        def body(i, _):
            pair = buf[pl.ds(start + 2 * i, 2)]
            wide = jnp.concatenate([pair[0], pair[1]], axis=1)
            value = dot(tab[tbl], jnp.concatenate([wide, wide], axis=0))
            result[2 * i] = value[:, :C]
            result[2 * i + 1] = value[:, C:]
            return 0

        lax.fori_loop(0, count // 2, body, 0)

    def inverse(rows, values):
        high = values.astype(BF16)
        low = (values - high.astype(F32)).astype(BF16)
        vh, vl = tab[2, rows, :], tab[3, rows, :]
        return dot(vh, high) + dot(vh, low) + dot(vl, high)

    def tile(f):
        return pl.ds(pl.multiple_of(8 * f, 8), 8), pl.ds(pl.multiple_of(T + 8 * f, 8), 8)

    sends = []
    waits, sent = spread(sig_v, xbuf, 8, 1, za_s, za_r, yf_s, yf_r, xh_s, xh_r)
    sends.append((waits, sent))
    transform(0, xbuf, 1 + y, REL, spec)

    def forward_tile(f, _):
        re, im = tile(f)
        for zp in range(Q):
            acc_r = jnp.zeros((8, C), F32)
            acc_i = jnp.zeros((8, C), F32)
            for d in range(LAGS):
                r = 7 + 4 * zp - d
                live = early[zp][d]
                s_r, s_i = spec[r, re, :] * live, spec[r, im, :] * live
                acc_r += kr[d, re, :] * s_r - ki[d, re, :] * s_i
                acc_i += kn[d, re, :] * s_i + ki[d, re, :] * s_r
            prod[re, zp * C : (zp + 1) * C] = acc_r
            prod[im, zp * C : (zp + 1) * C] = acc_i
        return 0

    lax.fori_loop(0, T // 8, forward_tile, 0)

    def give_back(rows, sbuf, rbuf, ssem, rsem):
        value = inverse(rows, prod[...]).astype(BF16)
        for zp in range(Q):
            sbuf[zp] = value[:, zp * C : (zp + 1) * C]
        copies = []
        for k in (2, 1, 3):
            copy = send(sbuf.at[lax.rem(z + k, Q)], rbuf.at[z], ssem.at[k - 1], rsem.at[k - 1], at(x, z + k, y))
            copy.start()
            copies.append(copy)
        rbuf[z] = sbuf[z]
        return copies

    copies = give_back(slice(T, 2 * T), conv_s, conv_r, zb_s, zb_r)
    for k in (1, 3, 2):
        copies[(2, 1, 3).index(k)].wait_recv()
    sends.append((copies, []))

    squares = jnp.zeros((T, C), F32)
    dots = jnp.zeros((T, C), F32)
    for j in range(Q):
        cols = slice(j * C, (j + 1) * C)
        mixed = conv_r[j].astype(F32) + skip[:, cols] * sig_v[:, cols].astype(F32)
        zval[:, cols] = mixed
        gated = gate_v[:, cols].astype(F32) * mixed
        squares += gated * gated
        dots += cot_v[:, cols].astype(F32) * gated

    ones = jnp.ones((8, C), BF16)

    def row_sums(values):
        total = jnp.zeros((8, T), F32)
        for _ in range(3):
            part = values.astype(BF16)
            total += lax.dot_general(ones, part, (((1,), (1,)), ((), ())), preferred_element_type=F32)
            values = values - part.astype(F32)
        return total

    upper = lax.broadcasted_iota(jnp.int32, (8, T), 0) < 4
    tpbuf[0] = jnp.where(upper, row_sums(squares), row_sums(dots))
    copies = []
    for k in range(1, 8):
        copy = send(tpbuf.at[0], tpbuf.at[k], tp_s.at[k - 1], tp_r.at[k - 1], (seq, lax.rem(tpi + k, 8)))
        copy.start()
        copies.append(copy)
    for copy in copies:
        copy.wait_recv()
    sends.append((copies, []))
    total = jnp.zeros((8, T), F32)
    for k in range(8):
        total += tpbuf[lax.rem(tpi + 8 - k, 8)]
    mean = total / (4 * C * 8)
    inv_row = lax.rsqrt(mean[0:1] + EPSILON)
    fac_row = mean[4:5] * inv_row * inv_row * inv_row
    inv = jnp.broadcast_to(inv_row, (T, T)).T
    fac = jnp.broadcast_to(fac_row, (T, T)).T
    for j in range(Q):
        cols = slice(j * C, (j + 1) * C)
        mixed = zval[:, cols]
        gate_f = gate_v[:, cols].astype(F32)
        gated = gate_f * mixed
        dgated = cot_v[:, cols].astype(F32) * inv - gated * fac
        dz[:, cols] = (dgated * gate_f).astype(BF16)
        out[:, cols] = (gated * inv).astype(BF16)
        ggate[:, cols] = (dgated * mixed).astype(BF16)

    waits, sent = spread(dz, dbuf, 0, 3, da_s, da_r, df_s, df_r, dh_s, dh_r)
    sends.append((waits, sent))
    transform(1, dbuf, y, REL, dspec)

    def filter_tile(f, _):
        re, im = tile(f)
        first = (lax.broadcasted_iota(jnp.int32, (8, C), 0) == 0) & (f == 0)
        sign = (1 - 2 * (lax.broadcasted_iota(jnp.int32, (8, C), 0) % 2)).astype(F32)
        own = []
        for zp in range(Q):
            d_r, d_i = dspec[4 * zp, re, :], dspec[4 * zp, im, :]
            own.append((d_r, jnp.where(first, 0.0, d_i), jnp.where(first, -d_i, d_r)))
        prior = None
        for d in range(LAGS):
            acc_r = jnp.zeros((8, C), F32)
            acc_i = jnp.zeros((8, C), F32)
            for zp in range(Q):
                r = 7 + 4 * zp - d
                live = early[zp][d]
                s_r, s_i = spec[r, re, :] * live, spec[r, im, :] * live
                d_r, d_i, d_n = own[zp]
                acc_r += d_r * s_r + d_i * s_i
                acc_i += d_i * s_r - d_n * s_i
            if prior is not None:
                cols = slice((d - 1) * C, d * C)
                gprod[re, cols] = prior[0] * sign + acc_r
                gprod[im, cols] = prior[1] * sign + acc_i
            prior = (acc_r, acc_i)
        cols = slice((LAGS - 1) * C, LAGS * C)
        gprod[re, cols] = prior[0] * sign
        gprod[im, cols] = prior[1] * sign
        return 0

    lax.fori_loop(0, T // 8, filter_tile, 0)
    scale = float(64 * T) ** (-0.5)
    for d in range(LAGS):
        value = inverse(slice(0, T), gprod[:, d * C : (d + 1) * C]) * scale
        for i in range(8):
            gf_s[i % 4, (d // 2) * 4 + 2 * (d % 2) + i // 4] = value[16 * i : 16 * i + 16].astype(BF16)
    gy_copies = []
    for k in (2, 1, 3):
        copy = send(gf_s.at[lax.rem(y + k, Q)], gf_r.at[k - 1], gy_ss.at[k - 1], gy_rs.at[k - 1], at(x, z, y + k))
        copy.start()
        gy_copies.append(copy)

    def backward_tile(f, _):
        re, im = tile(f)
        for zp in range(Q):
            acc_r = jnp.zeros((8, C), F32)
            acc_i = jnp.zeros((8, C), F32)
            for d in range(LAGS):
                r = 4 * zp + d
                live = late[zp][d]
                s_r, s_i = dspec[r, re, :] * live, dspec[r, im, :] * live
                acc_r += kr[d, re, :] * s_r + ki[d, re, :] * s_i
                acc_i += kn[d, re, :] * s_i - ki[d, re, :] * s_r
            prod[re, zp * C : (zp + 1) * C] = acc_r
            prod[im, zp * C : (zp + 1) * C] = acc_i
        return 0

    lax.fori_loop(0, T // 8, backward_tile, 0)
    back_copies = give_back(slice(0, T), back_s, back_r, db_s, db_r)
    sends.append((back_copies, []))

    for copy in gy_copies:
        copy.wait_recv()
    sends.append((gy_copies, []))
    gx_s[...] = (
        gf_s[y].astype(F32) + gf_r[0].astype(F32) + gf_r[1].astype(F32) + gf_r[2].astype(F32)
    ).reshape(Q, 4, 16, C)
    gx_copies = []
    for k in (2, 1, 3):
        copy = send(gx_s.at[lax.rem(x + k, Q)], gx_r.at[k - 1], gx_ss.at[k - 1], gx_rs.at[k - 1], at(x + k, z, y))
        copy.start()
        gx_copies.append(copy)
    for copy in gx_copies:
        copy.wait_recv()
    sends.append((gx_copies, []))
    gz_s[...] = gx_s[x] + gx_r[0] + gx_r[1] + gx_r[2]
    gz_copies = []
    for k in (2, 1, 3):
        copy = send(gz_s.at[lax.rem(z + k, Q)], gz_r.at[z], gz_ss.at[k - 1], gz_rs.at[k - 1], at(x, z + k, y))
        copy.start()
        gz_copies.append(copy)
    sends.append((gz_copies, []))
    gz_r[z] = gz_s[z]

    for copy in back_copies:
        copy.wait_recv()
    for j in range(Q):
        cols = slice(j * C, (j + 1) * C)
        gsig[:, cols] = (back_r[j].astype(F32) + skip[:, cols] * dz[:, cols].astype(F32)).astype(BF16)
    for copy in gz_copies:
        copy.wait_recv()
    for j in range(Q):
        gfilt[:, j * C : (j + 1) * C] = gz_r[j]

    for copies, conditional in sends:
        for copy in copies:
            copy.wait_send()
        for needed, copy in conditional:
            pl.when(needed)(copy.wait_send)


def on_device(signal, gate_input, filters, skip_weight, doc_lengths, grad_out):
    channels = signal.shape[1]
    vmem, anywhere = pl.BlockSpec(memory_space=pltpu.VMEM), pl.BlockSpec(memory_space=pl.ANY)
    dma = lambda *shape: pltpu.SemaphoreType.DMA(shape)
    block = (T, channels)
    scratch = [
        pltpu.VMEM(block, BF16), pltpu.VMEM(block, BF16), pltpu.VMEM(block, BF16),
        pltpu.VMEM((LAGS * T, C), BF16), pltpu.VMEM((4, 2 * T, 2 * T), BF16),
        pltpu.VMEM((24, T, C), BF16), pltpu.VMEM((24, T, C), BF16),
        pltpu.VMEM((REL, 2 * T, C), F32), pltpu.VMEM((REL, 2 * T, C), F32),
        pltpu.VMEM((LAGS, T, C), F32), pltpu.VMEM((LAGS, T, C), F32), pltpu.VMEM((LAGS, T, C), F32),
        pltpu.VMEM((2 * T, Q * C), F32), pltpu.VMEM((2 * T, LAGS * C), F32),
        pltpu.VMEM((Q, T, C), BF16), pltpu.VMEM((Q, T, C), BF16),
        pltpu.VMEM((Q, T, C), BF16), pltpu.VMEM((Q, T, C), BF16),
        pltpu.VMEM(block, F32), pltpu.VMEM(block, BF16), pltpu.VMEM((8, 8, T), F32),
        pltpu.VMEM((Q, 16, 16, C), BF16), pltpu.VMEM((3, 16, 16, C), BF16),
        pltpu.VMEM((Q, 4, 16, C), F32), pltpu.VMEM((3, 4, 16, C), F32),
        pltpu.VMEM((4, 16, C), F32), pltpu.VMEM((4, 16, C), F32),
        dma(5), dma(3), dma(3), dma(4, 3), dma(4, 3), dma(4, 4), dma(2, 4), dma(3), dma(3), dma(7), dma(7),
        dma(3), dma(3), dma(4, 3), dma(4, 3), dma(4, 4), dma(2, 4), dma(3), dma(3),
        dma(3), dma(3), dma(3), dma(3), dma(3), dma(3),
    ]
    out, gsig, ggate, gfilt = pl.pallas_call(
        kernel,
        out_shape=(
            jax.ShapeDtypeStruct(block, BF16), jax.ShapeDtypeStruct(block, BF16),
            jax.ShapeDtypeStruct(block, BF16), jax.ShapeDtypeStruct((16, channels), F32),
        ),
        in_specs=[pl.BlockSpec(memory_space=pltpu.SMEM), vmem] + [anywhere] * 5,
        out_specs=(vmem,) * 4,
        scratch_shapes=scratch,
        compiler_params=pltpu.CompilerParams(
            collective_id=0, has_side_effects=True, vmem_limit_bytes=48 << 20
        ),
        name="hyena",
    )(doc_lengths, skip_weight[None, :], signal, gate_input, filters, grad_out, jnp.asarray(tables()))
    return out, gsig, ggate, gfilt


def solution(mesh):
    placed = (P("seq", "tp"), P("seq", "tp"), P(None, "tp"), P("tp"), P(), P("seq", "tp"))
    return jax.shard_map(
        on_device,
        mesh=mesh,
        in_specs=placed,
        out_specs=(P("seq", "tp"), P("seq", "tp"), P("seq", "tp"), P("seq", "tp")),
        check_vma=False,
    )
```

```python
import functools
import math

import jax
import jax.numpy as jnp
import numpy as np
from jax import lax
from jax.experimental import pallas as pl
from jax.experimental.pallas import tpu as pltpu
from jax.sharding import PartitionSpec as P

EPSILON = 1e-06
MESH = pl.DeviceIdType.MESH
T = 128
C = 128
Q = 4
LAGS = 8
REL = 20
F32 = jnp.float32
BF16 = jnp.bfloat16


def tables():
    freq = np.arange(T)[:, None]
    time = np.arange(2 * T)[None, :]
    phase = (freq * time % (2 * T)) * (2.0 * math.pi / (2 * T))
    real, imag = np.cos(phase), -np.sin(phase)
    imag[0] = 1 - 2 * (np.arange(2 * T) % 2)
    forward = np.concatenate([real, imag], axis=0)
    scale = np.full((2 * T, 1), 1.0 / T)
    scale[0] = scale[T] = 0.5 / T
    backward = (forward * scale).T

    def split(table):
        table = table.astype(np.float32)
        high = table.astype(jnp.bfloat16)
        low = (table - high.astype(np.float32)).astype(jnp.bfloat16)
        return high, low

    high, low = split(forward)
    first = np.concatenate([high[:, :T], low[:, :T]], axis=1)
    second = np.concatenate([high[:, T:], low[:, T:]], axis=1)
    back_high, back_low = split(backward)
    return np.stack([first, second, back_high, back_low])


def dot(a, b):
    return jnp.dot(a, b, preferred_element_type=F32)


def kernel(
    docs, skip, signal, gate, filters, cotangent, table,
    out, gsig, ggate, gfilt,
    docs_v, late_m, skip_v, sig_v, gate_v, cot_v, taps, tab, xbuf, gbuf, cbuf, dbuf, rbuf, spec, dspec, kr, ki, kn,
    prod, gprod, zval, out_s, ggate_s, gsig_s, own_r, near_r, wide_s, wide_r,
    gf_s, gf_r, gy_s, gy_r, gz_s,
    inside_sem, load_sem, za_s, za_r, zr_s, zr_r, zf_s, zf_r, ga_s, ga_r, ca_s, ca_r, yf_s, yf_r, xh_s, xh_r, p_ss, p_rs, n_ss, n_rs, w_ss, w_rs,
    df_s, df_r, dh_s, dh_r, ob_s, ob_r, gb_s, gb_r, sb_s, sb_r, gx_ss, gx_rs, gy_ss, gy_rs, gz_ss, gz_rs,
):
    seq, tpi = lax.axis_index("seq"), lax.axis_index("tp")
    x, z, y = seq // 16, (seq // 4) % 4, seq % 4

    def at(xx, zz, yy):
        return (lax.rem(xx, Q) * 16 + lax.rem(zz, Q) * 4 + lax.rem(yy, Q), tpi)

    def send(src, dst, ssem, rsem, target):
        return pltpu.make_async_remote_copy(
            src_ref=src, dst_ref=dst, send_sem=ssem, recv_sem=rsem, device_id=target, device_id_type=MESH
        )

    barrier = pltpu.get_barrier_semaphore()
    partners = [at(x, z + k, y) for k in (1, 3)] + [at(x, z, y + k) for k in (1, 2, 3)]
    partners += [at(x + i, z, y + k) for i in (1, 3) for k in range(Q)] + [at(x + 2, z, y)]
    place, core = 4 * z + tpi // 2, lax.rem(tpi, 2)

    def ring(step, other):
        spot = lax.rem(place + step + 16, 16)
        return (16 * x + 4 * (spot // 4) + y, 2 * lax.rem(spot, 4) + lax.rem(core + other, 2))

    near = (8, 2, -2, 1, -1)
    wide = (5, -5)
    partners += [ring(step, 0) for step in near[1:]] + [ring(0, 1)]
    for partner in partners:
        pl.semaphore_signal(barrier, inc=1, device_id=partner, device_id_type=MESH)

    def chunk(k):
        return pl.ds(pl.multiple_of(lax.rem(k, Q) * C, C), C)

    lanes = chunk(z)
    own = 8 + 4 * z + y
    loads = [
        pltpu.make_async_copy(docs, docs_v, load_sem.at[0]),
        pltpu.make_async_copy(filters.at[:, lanes], taps, load_sem.at[1]),
        pltpu.make_async_copy(table, tab, load_sem.at[2]),
        pltpu.make_async_copy(signal, sig_v, load_sem.at[3]),
        pltpu.make_async_copy(signal.at[:, lanes], xbuf.at[own], load_sem.at[4]),
        pltpu.make_async_copy(gate.at[:, lanes], gbuf.at[z], load_sem.at[5]),
        pltpu.make_async_copy(cotangent.at[:, lanes], cbuf.at[z], load_sem.at[6]),
        pltpu.make_async_copy(skip.at[:, lanes], skip_v, load_sem.at[7]),
        pltpu.make_async_copy(gate, gate_v, load_sem.at[8]),
        pltpu.make_async_copy(cotangent, cot_v, load_sem.at[9]),
    ]
    for load in loads:
        load.start()

    for load in loads[3:]:
        load.wait()
    pl.semaphore_wait(barrier, len(partners))

    def along_z(source, target, ssem, rsem):
        copies = {}
        for k in (2, 1, 3):
            copies[k] = send(source.at[:, chunk(z + k)], target, ssem.at[k - 1], rsem.at[k - 1], at(x, z + k, y))
            copies[k].start()
        return copies

    def back_along_z(source, result, ssem, rsem):
        copies = {}
        for k in (2, 1, 3):
            copies[k] = send(
                source.at[lax.rem(z + k, Q)], result.at[:, lanes], ssem.at[k - 1], rsem.at[k - 1], at(x, z + k, y)
            )
            copies[k].start()
        result[:, lanes] = source[z]
        return copies

    def transform(tbl, buf, start, count, result):
        def body(i, _):
            pair = buf[pl.ds(start + 2 * i, 2)]
            wide = jnp.concatenate([pair[0], pair[1]], axis=1)
            value = dot(tab[tbl], jnp.concatenate([wide, wide], axis=0))
            result[start + 2 * i] = value[:, :C]
            result[start + 2 * i + 1] = value[:, C:]
            return 0

        lax.fori_loop(0, count // 2, body, 0)

    def inverse(rows, values):
        high = values.astype(BF16)
        low = (values - high.astype(F32)).astype(BF16)
        vh, vl = tab[2, rows, :], tab[3, rows, :]
        return dot(vh, high) + dot(vh, low) + dot(vl, high)

    def tile(f):
        return pl.ds(pl.multiple_of(8 * f, 8), 8), pl.ds(pl.multiple_of(T + 8 * f, 8), 8)

    waits = []
    halves = (pl.ds(0, T // 2), pl.ds(T // 2, T // 2))
    steps = (1, 3)
    relays = []
    for h, k in enumerate(steps):
        copy = send(sig_v.at[halves[h], chunk(z + 2)], rbuf.at[h], zr_s.at[h], zr_r.at[h], at(x, z + k, y))
        copy.start()
        relays.append(copy)
    for k in steps:
        copy = send(sig_v.at[:, chunk(z + k)], xbuf.at[own], za_s.at[k - 1], za_r.at[k - 1], at(x, z + k, y))
        copy.start()
        waits.append(copy)
    waits += relays
    for k in steps:
        pl.semaphore_signal(inside_sem, inc=1, device_id=at(x, z + k, y), device_id_type=MESH)
    sent = []
    late_loads = []

    def arrivals(zsrc):
        for j in (1, 2, 3):
            ysrc = lax.rem(y + 4 - j, Q)
            slot = xbuf.at[8 + 4 * zsrc + ysrc]
            copy = send(slot, slot, yf_s.at[0, j - 1], yf_r.at[zsrc, j - 1], at(x, z, ysrc))
            pl.when((zsrc < 3) | (y > ysrc))(copy.wait_recv)

    earlier = None
    for k in (0, 1, 3, 2):
        zsrc = lax.rem(z + 4 - k, Q)
        slot = xbuf.at[8 + 4 * zsrc + y]
        if k == 2:
            for h in range(2):
                half = slot.at[halves[h]]
                send(half, half, zf_s.at[h], zf_r.at[h], at(x, z + 2, y)).wait_recv()
        elif k:
            send(slot, slot, za_s.at[k - 1], za_r.at[k - 1], at(x, z + k, y)).wait_recv()
        for j in (2, 1, 3, 0):
            yp = lax.rem(y + j, Q)
            if j:
                needed = (zsrc < 3) | (yp > y)
                copy = send(slot, slot, yf_s.at[k, j - 1], yf_r.at[zsrc, j - 1], at(x, z, yp))
                pl.when(needed)(copy.start)
                sent.append((needed, copy))
            needed = (zsrc == 3) | ((zsrc == 2) & (yp < y))
            side = jnp.where(zsrc == 3, 1, 0)
            copy = send(slot, xbuf.at[4 * side + y], xh_s.at[k, j], xh_r.at[side, j], at(x + 1, z, yp))
            pl.when(needed)(copy.start)
            sent.append((needed, copy))
        if k == 0:
            loads[0].wait()
            early = []
            for zp in range(Q):
                block = 16 * x + 4 * zp + y
                begin, first, last = jnp.int32(0), jnp.int32(0), jnp.int32(0)
                for k in range(docs.shape[0]):
                    end = begin + docs_v[k]
                    inside = (begin <= block) & (block < end)
                    first = jnp.where(inside, begin, first)
                    last = jnp.where(inside, end, last)
                    begin = end
                early.append([jnp.where(block - d >= first, 1.0, 0.0).astype(F32) for d in range(LAGS)])
                for d in range(LAGS):
                    late_m[zp, d] = jnp.where(block + d < last, 1.0, 0.0).astype(F32)

            row0 = lax.broadcasted_iota(jnp.int32, (T, C), 0) == 0
            loads[1].wait()
            loads[2].wait()
            for d in range(LAGS):
                tap = taps[d * T : (d + 1) * T, :]
                value = dot(tab[1], jnp.concatenate([tap, tap], axis=0))
                if d > 0:
                    before = taps[(d - 1) * T : d * T, :]
                    value += dot(tab[0], jnp.concatenate([before, before], axis=0))
                real, imag = value[:T], value[T:]
                kr[d] = real
                ki[d] = jnp.where(row0, 0.0, imag)
                kn[d] = jnp.where(row0, imag, real)
            for h, step in enumerate(steps):
                relays[h].wait_recv()
                half = xbuf.at[8 + 4 * lax.rem(z + 4 - step, Q) + y].at[halves[h]]
                copy = send(rbuf.at[h], half, zf_s.at[h], zf_r.at[h], at(x, z + step, y))
                copy.start()
                waits.append(copy)
        if k == 1:
            pl.semaphore_wait(inside_sem, 2)
            g_copies = along_z(gate_v, gbuf.at[z], ga_s, ga_r)
            c_copies = along_z(cot_v, cbuf.at[z], ca_s, ca_r)
            waits += list(g_copies.values()) + list(c_copies.values())
        if earlier is not None:
            arrivals(earlier)
            transform(0, xbuf, 8 + 4 * earlier, 4, spec)
        earlier = zsrc
    arrivals(earlier)
    transform(0, xbuf, 8 + 4 * earlier, 4, spec)
    for side in (0, 1):
        for j in range(Q):
            ysrc = lax.rem(y + 4 - j, Q)
            slot = xbuf.at[4 * side + ysrc]
            copy = send(slot, slot, xh_s.at[0, j], xh_r.at[side, j], at(x + 3, z, ysrc))
            if side:
                copy.wait_recv()
            else:
                pl.when(y < ysrc)(copy.wait_recv)
    transform(0, xbuf, 0, 8, spec)

    def forward_tile(f, _):
        re, im = tile(f)
        for zp in range(Q):
            acc_r = jnp.zeros((8, C), F32)
            acc_i = jnp.zeros((8, C), F32)
            for d in range(LAGS):
                r = 8 + 4 * zp + y - d
                live = early[zp][d]
                s_r, s_i = spec[r, re, :] * live, spec[r, im, :] * live
                acc_r += kr[d, re, :] * s_r - ki[d, re, :] * s_i
                acc_i += kn[d, re, :] * s_i + ki[d, re, :] * s_r
            prod[re, zp * C : (zp + 1) * C] = acc_r
            prod[im, zp * C : (zp + 1) * C] = acc_i
        return 0

    lax.fori_loop(0, T // 8, forward_tile, 0)
    conv = inverse(slice(T, 2 * T), prod[...])
    for copies in (g_copies, c_copies):
        for k in (1, 3, 2):
            copies[k].wait_recv()

    ones = jnp.ones((2 * C, C), BF16)
    lane = lax.broadcasted_iota(jnp.int32, (T, C), 1)
    sums = jnp.zeros((T, C), F32)
    for zp in range(Q):
        mixed = conv[:, zp * C : (zp + 1) * C] + skip_v[...] * xbuf[8 + 4 * zp + y].astype(F32)
        zval[zp] = mixed
        gated = gbuf[zp].astype(F32) * mixed
        for number, values in ((zp, gated * gated), (Q + zp, cbuf[zp].astype(F32) * gated)):
            high = values.astype(BF16)
            low = (values - high.astype(F32)).astype(BF16)
            sums = jnp.where(lane == number, dot(jnp.concatenate([high, low], axis=1), ones), sums)
    own_r[0] = sums.T[:8]
    copy = send(own_r.at[0], own_r.at[1], p_ss.at[0], p_rs.at[0], ring(0, 1))
    copy.start()
    copy.wait()
    own_r[2] = own_r[0] + own_r[1]
    n_copies = []
    for i, step in enumerate(near):
        copy = send(own_r.at[2], near_r.at[i], n_ss.at[i], n_rs.at[i], ring(step, 0))
        copy.start()
        n_copies.append(copy)
    for copy in n_copies[1:]:
        copy.wait_recv()
    total = own_r[2] + ((near_r[1] + near_r[2]) + (near_r[3] + near_r[4]))
    wide_s[...] = total
    w_copies = []
    for i, step in enumerate(wide):
        copy = send(wide_s, wide_r.at[i], w_ss.at[i], w_rs.at[i], ring(step, 0))
        copy.start()
        w_copies.append(copy)
    for copy in n_copies[:1] + w_copies:
        copy.wait_recv()
    waits += n_copies + w_copies
    mean = (total + (wide_r[0] + wide_r[1]) + near_r[0]) / (Q * C * 8)
    inv_rows = lax.rsqrt(mean[0:4] + EPSILON)
    fac_rows = mean[4:8] * inv_rows * inv_rows * inv_rows
    factors = jnp.concatenate([inv_rows, fac_rows], axis=0).T

    d_sent = []
    for zp in range(Q):
        inv = jnp.broadcast_to(factors[:, zp : zp + 1], (T, C))
        fac = jnp.broadcast_to(factors[:, 4 + zp : 5 + zp], (T, C))
        mixed = zval[zp]
        gate_f = gbuf[zp].astype(F32)
        gated = gate_f * mixed
        dgated = cbuf[zp].astype(F32) * inv - gated * fac
        out_s[zp] = (gated * inv).astype(BF16)
        ggate_s[zp] = (dgated * mixed).astype(BF16)
        dbuf[zp, y] = (dgated * gate_f).astype(BF16)
        slot = dbuf.at[zp, y]
        for j in (2, 1, 3, 0):
            yp = lax.rem(y + j, Q)
            if j:
                needed = (y > yp) if zp == 0 else None
                copy = send(slot, slot, df_s.at[zp, j - 1], df_r.at[zp, j - 1], at(x, z, yp))
                d_sent.append((needed, copy))
            if zp < 2:
                needed = (yp > y) if zp == 1 else None
                copy = send(slot, dbuf.at[4 + zp, y], dh_s.at[zp, j], dh_r.at[zp, j], at(x + 3, z, yp))
                d_sent.append((needed, copy))
        for needed, copy in d_sent[len(d_sent) - (7 if zp < 2 else 3) :]:
            if needed is None:
                copy.start()
            else:
                pl.when(needed)(copy.start)
    for needed, copy in d_sent:
        sent.append((needed, copy))

    own_d = jnp.concatenate([dbuf[zp, y] for zp in range(Q)], axis=1)
    own_spec = dot(tab[1], jnp.concatenate([own_d, own_d], axis=0))
    for zp in range(Q):
        dspec[4 * zp + y] = own_spec[:, zp * C : (zp + 1) * C]

    def filter_tile(f, _):
        re, im = tile(f)
        first = (lax.broadcasted_iota(jnp.int32, (8, C), 0) == 0) & (f == 0)
        sign = (1 - 2 * (lax.broadcasted_iota(jnp.int32, (8, C), 0) % 2)).astype(F32)
        mine = []
        for zp in range(Q):
            d_r, d_i = dspec[4 * zp + y, re, :], dspec[4 * zp + y, im, :]
            mine.append((d_r, jnp.where(first, 0.0, d_i), jnp.where(first, -d_i, d_r)))
        prior = None
        for d in range(LAGS):
            acc_r = jnp.zeros((8, C), F32)
            acc_i = jnp.zeros((8, C), F32)
            for zp in range(Q):
                r = 8 + 4 * zp + y - d
                live = early[zp][d]
                s_r, s_i = spec[r, re, :] * live, spec[r, im, :] * live
                d_r, d_i, d_n = mine[zp]
                acc_r += d_r * s_r + d_i * s_i
                acc_i += d_i * s_r - d_n * s_i
            if prior is not None:
                cols = slice((d - 1) * C, d * C)
                gprod[re, cols] = prior[0] * sign + acc_r
                gprod[im, cols] = prior[1] * sign + acc_i
            prior = (acc_r, acc_i)
        cols = slice((LAGS - 1) * C, LAGS * C)
        gprod[re, cols] = prior[0] * sign
        gprod[im, cols] = prior[1] * sign
        return 0

    lax.fori_loop(0, T // 8, filter_tile, 0)
    scale = float(64 * T) ** (-0.5)
    for d in range(LAGS):
        value = inverse(slice(0, T), gprod[:, d * C : (d + 1) * C]) * scale
        for i in range(8):
            gf_s[d // 2, (i % 4) * 4 + 2 * (d % 2) + i // 4] = value[16 * i : 16 * i + 16].astype(BF16)
    gx_copies = []
    for k in (2, 1, 3):
        copy = send(gf_s.at[lax.rem(x + k, Q)], gf_r.at[k - 1], gx_ss.at[k - 1], gx_rs.at[k - 1], at(x + k, z, y))
        copy.start()
        gx_copies.append(copy)
    waits += gx_copies
    o_copies = back_along_z(out_s, out, ob_s, ob_r)
    gg_copies = back_along_z(ggate_s, ggate, gb_s, gb_r)

    def spectra(blocks, slots):
        wide_d = jnp.concatenate(blocks, axis=1)
        value = dot(tab[1], jnp.concatenate([wide_d, wide_d], axis=0))
        for k, slot in enumerate(slots):
            dspec[slot] = value[:, k * C : (k + 1) * C]

    for j in (1, 3, 2):
        ysrc = lax.rem(y + 4 - j, Q)
        for zp in range(Q):
            slot = dbuf.at[zp, ysrc]
            copy = send(slot, slot, df_s.at[zp, j - 1], df_r.at[zp, j - 1], at(x, z, ysrc))
            if zp == 0:
                pl.when(ysrc > y)(copy.wait_recv)
            else:
                copy.wait_recv()
        spectra([dbuf[zp, ysrc] for zp in range(Q)], [4 * zp + ysrc for zp in range(Q)])
    for j in (0, 1, 3, 2):
        ysrc = lax.rem(y + 4 - j, Q)
        for zp in range(2):
            slot = dbuf.at[4 + zp, ysrc]
            copy = send(slot, slot, dh_s.at[zp, j], dh_r.at[zp, j], at(x + 1, z, ysrc))
            if zp == 1:
                pl.when(y > ysrc)(copy.wait_recv)
            else:
                copy.wait_recv()
        spectra([dbuf[4 + zp, ysrc] for zp in range(2)], [16 + 4 * zp + ysrc for zp in range(2)])

    s_copies = {}
    for k in (2, 1, 3, 0):
        zp = lax.rem(z + k, Q)

        def backward_tile(f, _):
            re, im = tile(f)
            acc_r = jnp.zeros((8, C), F32)
            acc_i = jnp.zeros((8, C), F32)
            for d in range(LAGS):
                r = 4 * zp + y + d
                live = late_m[zp, d]
                s_r, s_i = dspec[r, re, :] * live, dspec[r, im, :] * live
                acc_r += kr[d, re, :] * s_r + ki[d, re, :] * s_i
                acc_i += kn[d, re, :] * s_i - ki[d, re, :] * s_r
            prod[re, :C] = acc_r
            prod[im, :C] = acc_i
            return 0

        lax.fori_loop(0, T // 8, backward_tile, 0)
        conv = inverse(slice(0, T), prod[:, :C])
        gsig_s[zp] = (conv + skip_v[...] * dbuf[zp, y].astype(F32)).astype(BF16)
        if k:
            s_copies[k] = send(gsig_s.at[zp], gsig.at[:, lanes], sb_s.at[k - 1], sb_r.at[k - 1], at(x, zp, y))
            s_copies[k].start()
    gsig[:, lanes] = gsig_s[z]

    for copy in gx_copies:
        copy.wait_recv()
    gy_s[...] = (
        gf_s[x].astype(F32) + gf_r[0].astype(F32) + gf_r[1].astype(F32) + gf_r[2].astype(F32)
    ).reshape(Q, 4, 16, C)
    gy_copies = []
    for k in (2, 1, 3):
        copy = send(gy_s.at[lax.rem(y + k, Q)], gy_r.at[k - 1], gy_ss.at[k - 1], gy_rs.at[k - 1], at(x, z, y + k))
        copy.start()
        gy_copies.append(copy)
    waits += gy_copies

    for copy in gy_copies:
        copy.wait_recv()
    gz_s[...] = gy_s[y] + gy_r[0] + gy_r[1] + gy_r[2]
    gz_copies = back_along_z(gz_s, gfilt, gz_ss, gz_rs)

    for copies in (o_copies, gg_copies, s_copies, gz_copies):
        for copy in copies.values():
            copy.wait()
    for copy in waits:
        copy.wait_send()
    for needed, copy in sent:
        if needed is None:
            copy.wait_send()
        else:
            pl.when(needed)(copy.wait_send)


def finish(a, b, c, d, e, f, g, h, sems):
    copies = [pltpu.make_async_copy(s, t, sems.at[i]) for i, (s, t) in enumerate(((a, e), (b, f), (c, g), (d, h)))]
    for copy in copies:
        copy.start()
    for copy in copies:
        copy.wait()


def on_device(signal, gate_input, filters, skip_weight, doc_lengths, grad_out):
    channels = signal.shape[1]
    vmem, hbm = pl.BlockSpec(memory_space=pltpu.VMEM), pl.BlockSpec(memory_space=pltpu.HBM)
    dma = lambda *shape: pltpu.SemaphoreType.DMA(shape)
    block = (T, channels)
    three = [dma(3)] * 2
    scratch = [
        pltpu.SMEM(doc_lengths.shape, jnp.int32), pltpu.SMEM((Q, LAGS), F32),
        pltpu.VMEM((1, C), F32),
        pltpu.VMEM(block, BF16), pltpu.VMEM(block, BF16), pltpu.VMEM(block, BF16),
        pltpu.VMEM((LAGS * T, C), BF16), pltpu.VMEM((4, 2 * T, 2 * T), BF16),
        pltpu.VMEM((24, T, C), BF16), pltpu.VMEM((Q, T, C), BF16), pltpu.VMEM((Q, T, C), BF16),
        pltpu.VMEM((6, Q, T, C), BF16), pltpu.VMEM((2, T // 2, C), BF16),
        pltpu.VMEM((24, 2 * T, C), F32), pltpu.VMEM((24, 2 * T, C), F32),
        pltpu.VMEM((LAGS, T, C), F32), pltpu.VMEM((LAGS, T, C), F32), pltpu.VMEM((LAGS, T, C), F32),
        pltpu.VMEM((2 * T, Q * C), F32), pltpu.VMEM((2 * T, LAGS * C), F32), pltpu.VMEM((Q, T, C), F32),
        pltpu.VMEM((Q, T, C), BF16), pltpu.VMEM((Q, T, C), BF16), pltpu.VMEM((Q, T, C), BF16),
        pltpu.VMEM((3, 8, T), F32), pltpu.VMEM((5, 8, T), F32),
        pltpu.VMEM((8, T), F32), pltpu.VMEM((2, 8, T), F32),
        pltpu.VMEM((Q, 16, 16, C), BF16), pltpu.VMEM((3, 16, 16, C), BF16),
        pltpu.VMEM((Q, 4, 16, C), F32), pltpu.VMEM((3, 4, 16, C), F32), pltpu.VMEM((4, 16, C), F32),
        pltpu.SemaphoreType.REGULAR, dma(10), *three, dma(2), dma(2), dma(2), dma(2), *three, *three, dma(4, 3), dma(4, 3), dma(4, 4), dma(2, 4), dma(1), dma(1), dma(5), dma(5), dma(2), dma(2),
        dma(4, 3), dma(4, 3), dma(2, 4), dma(2, 4), *three, *three, *three, *three, *three, *three,
    ]
    shapes = (
        jax.ShapeDtypeStruct(block, BF16), jax.ShapeDtypeStruct(block, BF16),
        jax.ShapeDtypeStruct(block, BF16), jax.ShapeDtypeStruct((16, channels), F32),
    )
    results = pl.pallas_call(
        kernel,
        out_shape=shapes,
        in_specs=[hbm] * 7,
        out_specs=(vmem,) * 4,
        scratch_shapes=scratch,
        compiler_params=pltpu.CompilerParams(
            collective_id=0, has_side_effects=True, vmem_limit_bytes=63 << 20
        ),
        name="hyena",
    )(doc_lengths, skip_weight[None, :], signal, gate_input, filters, grad_out, jnp.asarray(tables()))
    return pl.pallas_call(
        finish,
        out_shape=shapes,
        in_specs=[vmem] * 4,
        out_specs=(hbm,) * 4,
        scratch_shapes=[dma(4)],
        name="finish",
    )(*results)


def solution(mesh):
    placed = (P("seq", "tp"), P("seq", "tp"), P(None, "tp"), P("tp"), P(), P("seq", "tp"))
    return jax.shard_map(
        on_device,
        mesh=mesh,
        in_specs=placed,
        out_specs=(P("seq", "tp"), P("seq", "tp"), P("seq", "tp"), P("seq", "tp")),
        check_vma=False,
    )
```

```python
import functools
import math

import jax
import jax.numpy as jnp
import numpy as np
from jax import lax
from jax.experimental import pallas as pl
from jax.experimental.pallas import tpu as pltpu
from jax.sharding import PartitionSpec as P

EPSILON = 1e-06
MESH = pl.DeviceIdType.MESH
T = 128
C = 128
Q = 4
LAGS = 8
REL = 20
F32 = jnp.float32
BF16 = jnp.bfloat16


def tables():
    freq = np.arange(T)[:, None]
    time = np.arange(2 * T)[None, :]
    phase = (freq * time % (2 * T)) * (2.0 * math.pi / (2 * T))
    real, imag = np.cos(phase), -np.sin(phase)
    imag[0] = 1 - 2 * (np.arange(2 * T) % 2)
    forward = np.concatenate([real, imag], axis=0)
    scale = np.full((2 * T, 1), 1.0 / T)
    scale[0] = scale[T] = 0.5 / T
    backward = (forward * scale).T

    def split(table):
        table = table.astype(np.float32)
        high = table.astype(jnp.bfloat16)
        low = (table - high.astype(np.float32)).astype(jnp.bfloat16)
        return high, low

    high, low = split(forward)
    first = np.concatenate([high[:, :T], low[:, :T]], axis=1)
    second = np.concatenate([high[:, T:], low[:, T:]], axis=1)
    back_high, back_low = split(backward)
    return np.stack([first, second, back_high, back_low])


def dot(a, b):
    return jnp.dot(a, b, preferred_element_type=F32)


def kernel(
    docs, skip, signal, gate, filters, cotangent, table,
    out, gsig, ggate, gfilt,
    docs_v, late_m, skip_v, sig_v, gate_v, cot_v, taps, tab, xbuf, gbuf, cbuf, dbuf, rbuf, spec, dspec, kr, ki, kn,
    prod, gprod, zval, inv_b, fac_b, z_s, z_r, gsig_s, own_r, near_r, far_r, wide_s, wide_r,
    gf_s, gf_r, gz_s,
    inside_sem, load_sem, za_s, za_r, zr_s, zr_r, zf_s, zf_r, ga_s, ga_r, ca_s, ca_r, yf_s, yf_r, xh_s, xh_r, n_ss, n_rs, w_ss, w_rs,
    df_s, df_r, dh_s, dh_r, zb_s, zb_r, sb_s, sb_r, gx_ss, gx_rs, gz_ss, gz_rs,
):
    seq, tpi = lax.axis_index("seq"), lax.axis_index("tp")
    x, z, y = seq // 16, (seq // 4) % 4, seq % 4

    def at(xx, zz, yy):
        return (lax.rem(xx, Q) * 16 + lax.rem(zz, Q) * 4 + lax.rem(yy, Q), tpi)

    def send(src, dst, ssem, rsem, target):
        return pltpu.make_async_remote_copy(
            src_ref=src, dst_ref=dst, send_sem=ssem, recv_sem=rsem, device_id=target, device_id_type=MESH
        )

    barrier = pltpu.get_barrier_semaphore()
    partners = [at(x, z + k, y) for k in (1, 3)] + [at(x, z, y + k) for k in (1, 2, 3)]
    partners += [at(x + i, z, y + k) for i in (1, 3) for k in range(Q)] + [at(x + 2, z, y)]
    place, core = 4 * z + tpi // 2, lax.rem(tpi, 2)

    def ring(step, other):
        spot = lax.rem(place + step + 16, 16)
        return (16 * x + 4 * (spot // 4) + y, 2 * lax.rem(spot, 4) + lax.rem(core + other, 2))

    near = [(8, 0), (8, 1)] + [(step, other) for step in (2, -2, 1, -1) for other in (0, 1)] + [(0, 1)]
    wide = (5, -5)
    partners += [ring(step, other) for step, other in near[2:]]
    for partner in partners:
        pl.semaphore_signal(barrier, inc=1, device_id=partner, device_id_type=MESH)

    def chunk(k):
        return pl.ds(pl.multiple_of(lax.rem(k, Q) * C, C), C)

    lanes = chunk(z)
    own = 8 + 4 * z + y
    loads = [
        pltpu.make_async_copy(docs, docs_v, load_sem.at[0]),
        pltpu.make_async_copy(filters.at[:, lanes], taps, load_sem.at[1]),
        pltpu.make_async_copy(table, tab, load_sem.at[2]),
        pltpu.make_async_copy(signal, sig_v, load_sem.at[3]),
        pltpu.make_async_copy(signal.at[:, lanes], xbuf.at[own], load_sem.at[4]),
        pltpu.make_async_copy(gate.at[:, lanes], gbuf.at[z], load_sem.at[5]),
        pltpu.make_async_copy(cotangent.at[:, lanes], cbuf.at[z], load_sem.at[6]),
        pltpu.make_async_copy(skip.at[:, lanes], skip_v, load_sem.at[7]),
        pltpu.make_async_copy(gate, gate_v, load_sem.at[8]),
        pltpu.make_async_copy(cotangent, cot_v, load_sem.at[9]),
    ]
    for load in loads:
        load.start()

    for load in loads[3:]:
        load.wait()
    pl.semaphore_wait(barrier, len(partners))

    def along_z(source, target, ssem, rsem):
        copies = {}
        for k in (2, 1, 3):
            copies[k] = send(source.at[:, chunk(z + k)], target, ssem.at[k - 1], rsem.at[k - 1], at(x, z + k, y))
            copies[k].start()
        return copies

    def back_along_z(source, result, ssem, rsem):
        copies = {}
        for k in (2, 1, 3):
            copies[k] = send(
                source.at[lax.rem(z + k, Q)], result.at[:, lanes], ssem.at[k - 1], rsem.at[k - 1], at(x, z + k, y)
            )
            copies[k].start()
        result[:, lanes] = source[z]
        return copies

    def transform(tbl, buf, start, count, result):
        def body(i, _):
            pair = buf[pl.ds(start + 2 * i, 2)]
            wide = jnp.concatenate([pair[0], pair[1]], axis=1)
            value = dot(tab[tbl], jnp.concatenate([wide, wide], axis=0))
            result[start + 2 * i] = value[:, :C]
            result[start + 2 * i + 1] = value[:, C:]
            return 0

        lax.fori_loop(0, count // 2, body, 0)

    def inverse(rows, values):
        high = values.astype(BF16)
        low = (values - high.astype(F32)).astype(BF16)
        vh, vl = tab[2, rows, :], tab[3, rows, :]
        return dot(vh, high) + dot(vh, low) + dot(vl, high)

    def tile(f):
        return pl.ds(pl.multiple_of(8 * f, 8), 8), pl.ds(pl.multiple_of(T + 8 * f, 8), 8)

    waits = []
    halves = (pl.ds(0, T // 2), pl.ds(T // 2, T // 2))
    steps = (1, 3)
    relays = []
    for h, k in enumerate(steps):
        copy = send(sig_v.at[halves[h], chunk(z + 2)], rbuf.at[h], zr_s.at[h], zr_r.at[h], at(x, z + k, y))
        copy.start()
        relays.append(copy)
    for k in steps:
        copy = send(sig_v.at[:, chunk(z + k)], xbuf.at[own], za_s.at[k - 1], za_r.at[k - 1], at(x, z + k, y))
        copy.start()
        waits.append(copy)
    waits += relays
    for k in steps:
        pl.semaphore_signal(inside_sem, inc=1, device_id=at(x, z + k, y), device_id_type=MESH)
    sent = []
    late_loads = []

    def arrivals(zsrc):
        for j in (1, 2, 3):
            ysrc = lax.rem(y + 4 - j, Q)
            slot = xbuf.at[8 + 4 * zsrc + ysrc]
            copy = send(slot, slot, yf_s.at[0, j - 1], yf_r.at[zsrc, j - 1], at(x, z, ysrc))
            pl.when((zsrc < 3) | (y > ysrc))(copy.wait_recv)

    for k in (0, 1, 3, 2):
        zsrc = lax.rem(z + 4 - k, Q)
        slot = xbuf.at[8 + 4 * zsrc + y]
        if k == 2:
            for h in range(2):
                half = slot.at[halves[h]]
                send(half, half, zf_s.at[h], zf_r.at[h], at(x, z + 2, y)).wait_recv()
        elif k:
            send(slot, slot, za_s.at[k - 1], za_r.at[k - 1], at(x, z + k, y)).wait_recv()
        side = jnp.where(zsrc == 3, 1, 0)
        ways = [("y", j) for j in (2, 1, 3)]
        halo = [("x", j) for j in (2, 1, 3, 0)]
        for way, j in halo + ways if k == 2 else ways + halo:
            yp = lax.rem(y + j, Q)
            if way == "y":
                needed = (zsrc < 3) | (yp > y)
                copy = send(slot, slot, yf_s.at[k, j - 1], yf_r.at[zsrc, j - 1], at(x, z, yp))
            else:
                needed = (zsrc == 3) | ((zsrc == 2) & (yp < y))
                copy = send(slot, xbuf.at[4 * side + y], xh_s.at[k, j], xh_r.at[side, j], at(x + 1, z, yp))
            pl.when(needed)(copy.start)
            sent.append((needed, copy))
        if k == 0:
            for h, step in enumerate(steps):
                relays[h].wait_recv()
                half = xbuf.at[8 + 4 * lax.rem(z + 4 - step, Q) + y].at[halves[h]]
                copy = send(rbuf.at[h], half, zf_s.at[h], zf_r.at[h], at(x, z + step, y))
                copy.start()
                waits.append(copy)
        if k == 1:
            pl.semaphore_wait(inside_sem, 2)
            g_copies = along_z(gate_v, gbuf.at[z], ga_s, ga_r)
            c_copies = along_z(cot_v, cbuf.at[z], ca_s, ca_r)
            waits += list(g_copies.values()) + list(c_copies.values())
        if k == 3:
            loads[0].wait()
            early = []
            for zp in range(Q):
                block = 16 * x + 4 * zp + y
                begin, first, last = jnp.int32(0), jnp.int32(0), jnp.int32(0)
                for k in range(docs.shape[0]):
                    end = begin + docs_v[k]
                    inside = (begin <= block) & (block < end)
                    first = jnp.where(inside, begin, first)
                    last = jnp.where(inside, end, last)
                    begin = end
                early.append([jnp.where(block - d >= first, 1.0, 0.0).astype(F32) for d in range(LAGS)])
                for d in range(LAGS):
                    late_m[zp, d] = jnp.where(block + d < last, 1.0, 0.0).astype(F32)

            row0 = lax.broadcasted_iota(jnp.int32, (T, C), 0) == 0
            loads[1].wait()
            loads[2].wait()
            for d in range(LAGS):
                tap = taps[d * T : (d + 1) * T, :]
                value = dot(tab[1], jnp.concatenate([tap, tap], axis=0))
                if d > 0:
                    before = taps[(d - 1) * T : d * T, :]
                    value += dot(tab[0], jnp.concatenate([before, before], axis=0))
                real, imag = value[:T], value[T:]
                kr[d] = real
                ki[d] = jnp.where(row0, 0.0, imag)
                kn[d] = jnp.where(row0, imag, real)
            for step in (0, 1, 3):
                earlier = lax.rem(z + 4 - step, Q)
                arrivals(earlier)
                transform(0, xbuf, 8 + 4 * earlier, 4, spec)
    arrivals(zsrc)
    transform(0, xbuf, 8 + 4 * zsrc, 4, spec)
    for side in (0, 1):
        for j in range(Q):
            ysrc = lax.rem(y + 4 - j, Q)
            slot = xbuf.at[4 * side + ysrc]
            copy = send(slot, slot, xh_s.at[0, j], xh_r.at[side, j], at(x + 3, z, ysrc))
            if side:
                copy.wait_recv()
            else:
                pl.when(y < ysrc)(copy.wait_recv)
    transform(0, xbuf, 0, 8, spec)

    def forward_tile(f, _):
        re, im = tile(f)
        for zp in range(Q):
            acc_r = jnp.zeros((8, C), F32)
            acc_i = jnp.zeros((8, C), F32)
            for d in range(LAGS):
                r = 8 + 4 * zp + y - d
                live = early[zp][d]
                s_r, s_i = spec[r, re, :] * live, spec[r, im, :] * live
                acc_r += kr[d, re, :] * s_r - ki[d, re, :] * s_i
                acc_i += kn[d, re, :] * s_i + ki[d, re, :] * s_r
            prod[re, zp * C : (zp + 1) * C] = acc_r
            prod[im, zp * C : (zp + 1) * C] = acc_i
        return 0

    lax.fori_loop(0, T // 8, forward_tile, 0)
    conv = inverse(slice(T, 2 * T), prod[...])
    for copies in (g_copies, c_copies):
        for k in (1, 3, 2):
            copies[k].wait_recv()

    ones = jnp.ones((2 * C, C), BF16)
    lane = lax.broadcasted_iota(jnp.int32, (T, C), 1)
    sums = jnp.zeros((T, C), F32)
    for zp in range(Q):
        mixed = conv[:, zp * C : (zp + 1) * C] + skip_v[...] * xbuf[8 + 4 * zp + y].astype(F32)
        zval[zp] = mixed
        z_s[zp, 0] = mixed.astype(BF16)
        z_s[zp, 1] = (mixed - mixed.astype(BF16).astype(F32)).astype(BF16)
        gated = gbuf[zp].astype(F32) * mixed
        for number, values in ((zp, gated * gated), (Q + zp, cbuf[zp].astype(F32) * gated)):
            high = values.astype(BF16)
            low = (values - high.astype(F32)).astype(BF16)
            sums = jnp.where(lane == number, dot(jnp.concatenate([high, low], axis=1), ones), sums)
    own_r[...] = sums.T[:8]
    n_copies = []
    for i, (step, other) in enumerate(near):
        dst = far_r.at[i] if i < 2 else near_r.at[i - 2]
        copy = send(own_r, dst, n_ss.at[i], n_rs.at[i], ring(step, other))
        copy.start()
        n_copies.append(copy)
    for copy in n_copies[2:]:
        copy.wait_recv()
    total = own_r[...]
    for i in range(9):
        total += near_r[i]
    wide_s[...] = total
    w_copies = []
    for i, step in enumerate(wide):
        copy = send(wide_s, wide_r.at[i], w_ss.at[i], w_rs.at[i], ring(step, 0))
        copy.start()
        w_copies.append(copy)
    zb_copies = []
    for k in (2, 1, 3):
        copy = send(z_s.at[lax.rem(z + k, Q)], z_r.at[z], zb_s.at[k - 1], zb_r.at[k - 1], at(x, z + k, y))
        copy.start()
        zb_copies.append(copy)
    for copy in n_copies[:2] + w_copies:
        copy.wait_recv()
    waits += n_copies + w_copies
    mean = (total + (wide_r[0] + wide_r[1]) + (far_r[0] + far_r[1])) / (Q * C * 8)
    inv_rows = lax.rsqrt(mean[0:4] + EPSILON)
    fac_rows = mean[4:8] * inv_rows * inv_rows * inv_rows
    factors = jnp.concatenate([inv_rows, fac_rows], axis=0).T

    for zp in range(Q):
        inv = jnp.broadcast_to(factors[:, zp : zp + 1], (T, C))
        fac = jnp.broadcast_to(factors[:, 4 + zp : 5 + zp], (T, C))
        inv_b[zp] = inv
        fac_b[zp] = fac
        gate_f = gbuf[zp].astype(F32)
        dgated = cbuf[zp].astype(F32) * inv - gate_f * zval[zp] * fac
        dbuf[zp, y] = (dgated * gate_f).astype(BF16)

    def by_z(*values):
        result = jnp.int32(values[0])
        for number in range(1, Q):
            result = jnp.where(z == number, values[number], result)
        return result

    quads = [by_z(*row) for row in ((2, 3, 0, 1), (3, 4, 1, 2), (4, 5, 2, 3), (1, 2, 3, 0), (5, 0, 4, 4), (0, 1, 5, 5))]
    order = [by_z(*row) for row in ((2, 3, 0, 1), (1, 2, 1, 0), (3, 0, 3, 2), (0, 1, 2, 3))]

    def quad_copies(quad, way):
        result = []
        for j in (2, 1, 3, 0):
            other = lax.rem(y + Q + way * j, Q)
            source, target = (y, other) if way == 1 else (other, y)
            if j:
                own_quad = lax.rem(quad, Q)
                slot = dbuf.at[own_quad, source]
                copy = send(slot, slot, df_s.at[own_quad, j - 1], df_r.at[own_quad, j - 1], at(x, z, other))
                result.append(((quad < Q) & ((quad > 0) | (source > target)), copy))
            side = lax.rem(quad, 2)
            copy = send(
                dbuf.at[side, source], dbuf.at[4 + side, source], dh_s.at[side, j], dh_r.at[side, j],
                at(x + (3 if way == 1 else 1), z, other),
            )
            result.append(((quad == 4) | ((quad == 5) & (target > source)), copy))
        return result

    for quad in quads:
        for needed, copy in quad_copies(quad, 1):
            pl.when(needed)(copy.start)
            sent.append((needed, copy))

    own_d = jnp.concatenate([dbuf[zp, y] for zp in range(Q)], axis=1)
    own_spec = dot(tab[1], jnp.concatenate([own_d, own_d], axis=0))
    for zp in range(Q):
        dspec[4 * zp + y] = own_spec[:, zp * C : (zp + 1) * C]

    def filter_tile(f, _):
        re, im = tile(f)
        first = (lax.broadcasted_iota(jnp.int32, (8, C), 0) == 0) & (f == 0)
        sign = (1 - 2 * (lax.broadcasted_iota(jnp.int32, (8, C), 0) % 2)).astype(F32)
        mine = []
        for zp in range(Q):
            d_r, d_i = dspec[4 * zp + y, re, :], dspec[4 * zp + y, im, :]
            mine.append((d_r, jnp.where(first, 0.0, d_i), jnp.where(first, -d_i, d_r)))
        prior = None
        for d in range(LAGS):
            acc_r = jnp.zeros((8, C), F32)
            acc_i = jnp.zeros((8, C), F32)
            for zp in range(Q):
                r = 8 + 4 * zp + y - d
                live = early[zp][d]
                s_r, s_i = spec[r, re, :] * live, spec[r, im, :] * live
                d_r, d_i, d_n = mine[zp]
                acc_r += d_r * s_r + d_i * s_i
                acc_i += d_i * s_r - d_n * s_i
            if prior is not None:
                cols = slice((d - 1) * C, d * C)
                gprod[re, cols] = prior[0] * sign + acc_r
                gprod[im, cols] = prior[1] * sign + acc_i
            prior = (acc_r, acc_i)
        cols = slice((LAGS - 1) * C, LAGS * C)
        gprod[re, cols] = prior[0] * sign
        gprod[im, cols] = prior[1] * sign
        return 0

    lax.fori_loop(0, T // 8, filter_tile, 0)
    scale = float(64 * T) ** (-0.5)
    for half in range(Q):
        value = inverse(slice(0, T), gprod[:, 2 * half * C : 2 * (half + 1) * C]) * scale
        for odd in range(2):
            for i in range(8):
                piece = value[16 * i : 16 * i + 16, odd * C : (odd + 1) * C].astype(BF16)
                gf_s[half, i % 4, 2 * odd + i // 4] = piece
    gx_copies = []
    around = [(i, k) for i in (2, 1, 3, 0) for k in (2, 1, 3, 0) if i or k]
    for n, (i, k) in enumerate(around):
        copy = send(
            gf_s.at[lax.rem(x + i, Q), lax.rem(y + k, Q)], gf_r.at[n], gx_ss.at[n], gx_rs.at[n], at(x + i, z, y + k)
        )
        copy.start()
        gx_copies.append(copy)
    waits += gx_copies

    def arrive(quad):
        for needed, copy in quad_copies(quad, -1):
            pl.when(needed)(copy.wait_recv)
        blocks = jnp.concatenate([dbuf[quad, k] for k in range(Q)], axis=1)
        value = dot(tab[1], jnp.concatenate([blocks, blocks], axis=0))
        for k in range(Q):
            dspec[4 * quad + k] = value[:, k * C : (k + 1) * C]

    def signal_gradient(zp):
        def backward_tile(f, _):
            re, im = tile(f)
            acc_r = jnp.zeros((8, C), F32)
            acc_i = jnp.zeros((8, C), F32)
            for d in range(LAGS):
                r = 4 * zp + y + d
                live = late_m[zp, d]
                s_r, s_i = dspec[r, re, :] * live, dspec[r, im, :] * live
                acc_r += kr[d, re, :] * s_r + ki[d, re, :] * s_i
                acc_i += kn[d, re, :] * s_i - ki[d, re, :] * s_r
            prod[re, :C] = acc_r
            prod[im, :C] = acc_i
            return 0

        lax.fori_loop(0, T // 8, backward_tile, 0)
        conv = inverse(slice(0, T), prod[:, :C])
        gsig_s[zp] = (conv + skip_v[...] * dbuf[zp, y].astype(F32)).astype(BF16)

    s_copies = []

    def give(number):
        zp = order[number]
        step = lax.rem(zp + Q - z, Q) - 1
        signal_gradient(zp)
        copy = send(gsig_s.at[zp], gsig.at[:, lanes], sb_s.at[step], sb_r.at[step], at(x, zp, y))
        copy.start()
        s_copies.append(copy)

    for quad in quads[:3]:
        arrive(quad)
    give(0)
    arrive(quads[3])
    give(1)

    arrive(quads[4])
    arrive(quads[5])
    give(2)

    for copy in gx_copies:
        copy.wait_recv()
    total = gf_s[x, y].astype(F32)
    for n in range(len(around)):
        total += gf_r[n].astype(F32)
    gz_s[...] = total
    gz_copies = back_along_z(gz_s, gfilt, gz_ss, gz_rs)
    signal_gradient(z)
    gsig[:, lanes] = gsig_s[z]

    z_r[z] = z_s[z]
    for copy in zb_copies:
        copy.wait()
    inv, fac = inv_b[z], fac_b[z]
    for j in range(Q):
        cols = slice(j * C, (j + 1) * C)
        mixed = z_r[j, 0].astype(F32) + z_r[j, 1].astype(F32)
        gated = gate_v[:, cols].astype(F32) * mixed
        dgated = cot_v[:, cols].astype(F32) * inv - gated * fac
        out[:, cols] = (gated * inv).astype(BF16)
        ggate[:, cols] = (dgated * mixed).astype(BF16)

    for copy in s_copies:
        copy.wait()
    for copy in gz_copies.values():
        copy.wait()
    for copy in waits:
        copy.wait_send()
    for needed, copy in sent:
        if needed is None:
            copy.wait_send()
        else:
            pl.when(needed)(copy.wait_send)


def finish(a, b, c, d, e, f, g, h, sems):
    copies = [pltpu.make_async_copy(s, t, sems.at[i]) for i, (s, t) in enumerate(((a, e), (b, f), (c, g), (d, h)))]
    for copy in copies:
        copy.start()
    for copy in copies:
        copy.wait()


def on_device(signal, gate_input, filters, skip_weight, doc_lengths, grad_out):
    channels = signal.shape[1]
    vmem, hbm = pl.BlockSpec(memory_space=pltpu.VMEM), pl.BlockSpec(memory_space=pltpu.HBM)
    dma = lambda *shape: pltpu.SemaphoreType.DMA(shape)
    block = (T, channels)
    three = [dma(3)] * 2
    scratch = [
        pltpu.SMEM(doc_lengths.shape, jnp.int32), pltpu.SMEM((Q, LAGS), F32),
        pltpu.VMEM((1, C), F32),
        pltpu.VMEM(block, BF16), pltpu.VMEM(block, BF16), pltpu.VMEM(block, BF16),
        pltpu.VMEM((LAGS * T, C), BF16), pltpu.VMEM((4, 2 * T, 2 * T), BF16),
        pltpu.VMEM((24, T, C), BF16), pltpu.VMEM((Q, T, C), BF16), pltpu.VMEM((Q, T, C), BF16),
        pltpu.VMEM((6, Q, T, C), BF16), pltpu.VMEM((2, T // 2, C), BF16),
        pltpu.VMEM((24, 2 * T, C), F32), pltpu.VMEM((24, 2 * T, C), F32),
        pltpu.VMEM((LAGS, T, C), F32), pltpu.VMEM((LAGS, T, C), F32), pltpu.VMEM((LAGS, T, C), F32),
        pltpu.VMEM((2 * T, Q * C), F32), pltpu.VMEM((2 * T, LAGS * C), F32), pltpu.VMEM((Q, T, C), F32),
        pltpu.VMEM((Q, T, C), F32), pltpu.VMEM((Q, T, C), F32),
        pltpu.VMEM((Q, 2, T, C), BF16), pltpu.VMEM((Q, 2, T, C), BF16), pltpu.VMEM((Q, T, C), BF16),
        pltpu.VMEM((8, T), F32), pltpu.VMEM((9, 8, T), F32), pltpu.VMEM((2, 8, T), F32),
        pltpu.VMEM((8, T), F32), pltpu.VMEM((2, 8, T), F32),
        pltpu.VMEM((Q, Q, 4, 16, C), BF16), pltpu.VMEM((15, 4, 16, C), BF16), pltpu.VMEM((4, 16, C), F32),
        pltpu.SemaphoreType.REGULAR, dma(10), *three, dma(2), dma(2), dma(2), dma(2), *three, *three, dma(4, 3), dma(4, 3), dma(4, 4), dma(2, 4), dma(11), dma(11), dma(2), dma(2),
        dma(4, 3), dma(4, 3), dma(2, 4), dma(2, 4), *three, *three, dma(15), dma(15), *three,
    ]
    shapes = (
        jax.ShapeDtypeStruct(block, BF16), jax.ShapeDtypeStruct(block, BF16),
        jax.ShapeDtypeStruct(block, BF16), jax.ShapeDtypeStruct((16, channels), F32),
    )
    results = pl.pallas_call(
        kernel,
        out_shape=shapes,
        in_specs=[hbm] * 7,
        out_specs=(vmem,) * 4,
        scratch_shapes=scratch,
        compiler_params=pltpu.CompilerParams(
            collective_id=0, has_side_effects=True, vmem_limit_bytes=63 << 20
        ),
        name="hyena",
    )(doc_lengths, skip_weight[None, :], signal, gate_input, filters, grad_out, jnp.asarray(tables()))
    return pl.pallas_call(
        finish,
        out_shape=shapes,
        in_specs=[vmem] * 4,
        out_specs=(hbm,) * 4,
        scratch_shapes=[dma(4)],
        name="finish",
    )(*results)


def solution(mesh):
    placed = (P("seq", "tp"), P("seq", "tp"), P(None, "tp"), P("tp"), P(), P("seq", "tp"))
    return jax.shard_map(
        on_device,
        mesh=mesh,
        in_specs=placed,
        out_specs=(P("seq", "tp"), P("seq", "tp"), P("seq", "tp"), P("seq", "tp")),
        check_vma=False,
    )
```

```python
import functools
import math

import jax
import jax.numpy as jnp
import numpy as np
from jax import lax
from jax.experimental import pallas as pl
from jax.experimental.pallas import tpu as pltpu
from jax.sharding import PartitionSpec as P

EPSILON = 1e-06
MESH = pl.DeviceIdType.MESH
T = 128
C = 128
Q = 4
LAGS = 8
REL = 20
F32 = jnp.float32
BF16 = jnp.bfloat16


def tables():
    freq = np.arange(T)[:, None]
    time = np.arange(2 * T)[None, :]
    phase = (freq * time % (2 * T)) * (2.0 * math.pi / (2 * T))
    real, imag = np.cos(phase), -np.sin(phase)
    imag[0] = 1 - 2 * (np.arange(2 * T) % 2)
    forward = np.concatenate([real, imag], axis=0)
    scale = np.full((2 * T, 1), 1.0 / T)
    scale[0] = scale[T] = 0.5 / T
    backward = (forward * scale).T

    def split(table):
        table = table.astype(np.float32)
        high = table.astype(jnp.bfloat16)
        low = (table - high.astype(np.float32)).astype(jnp.bfloat16)
        return high, low

    high, low = split(forward)
    first = np.concatenate([high[:, :T], low[:, :T]], axis=1)
    second = np.concatenate([high[:, T:], low[:, T:]], axis=1)
    back_high, back_low = split(backward)
    return np.stack([first, second, back_high, back_low])


def dot(a, b):
    return jnp.dot(a, b, preferred_element_type=F32)


def kernel(
    docs, skip, signal, gate, filters, cotangent, table,
    out, gsig, ggate, gfilt,
    docs_v, late_m, skip_v, sig_v, gate_v, cot_v, taps, tab, xbuf, gbuf, cbuf, dbuf, rbuf, spec, dspec, kr, ki, kn,
    prod, gprod, zval, inv_b, fac_b, z_s, z_r, out_v, ggate_v, gsig_s, own_r, near_r, far_r, wide_s, wide_r,
    gf_s, gf_r, gz_s,
    inside_sem, load_sem, store_sem, za_s, za_r, zr_s, zr_r, zf_s, zf_r, ga_s, ga_r, ca_s, ca_r, yf_s, yf_r, xh_s, xh_r, n_ss, n_rs, w_ss, w_rs,
    df_s, df_r, dh_s, dh_r, zb_s, zb_r, sb_s, sb_r, gx_ss, gx_rs, gz_ss, gz_rs,
):
    seq, tpi = lax.axis_index("seq"), lax.axis_index("tp")
    x, z, y = seq // 16, (seq // 4) % 4, seq % 4

    def at(xx, zz, yy):
        return (lax.rem(xx, Q) * 16 + lax.rem(zz, Q) * 4 + lax.rem(yy, Q), tpi)

    def send(src, dst, ssem, rsem, target):
        return pltpu.make_async_remote_copy(
            src_ref=src, dst_ref=dst, send_sem=ssem, recv_sem=rsem, device_id=target, device_id_type=MESH
        )

    barrier = pltpu.get_barrier_semaphore()
    partners = [at(x, z + k, y) for k in (1, 3)] + [at(x, z, y + k) for k in (1, 2, 3)]
    partners += [at(x + i, z, y + k) for i in (1, 3) for k in range(Q)] + [at(x + 2, z, y)]
    place, core = 4 * z + tpi // 2, lax.rem(tpi, 2)

    def ring(step, other):
        spot = lax.rem(place + step + 16, 16)
        return (16 * x + 4 * (spot // 4) + y, 2 * lax.rem(spot, 4) + lax.rem(core + other, 2))

    near = [(8, 0), (8, 1)] + [(step, other) for step in (2, -2, 1, -1) for other in (0, 1)] + [(0, 1)]
    wide = (5, -5)
    partners += [ring(step, other) for step, other in near[2:]]
    for partner in partners:
        pl.semaphore_signal(barrier, inc=1, device_id=partner, device_id_type=MESH)

    def chunk(k):
        return pl.ds(pl.multiple_of(lax.rem(k, Q) * C, C), C)

    lanes = chunk(z)
    own = 8 + 4 * z + y
    loads = [
        pltpu.make_async_copy(docs, docs_v, load_sem.at[0]),
        pltpu.make_async_copy(filters.at[:, lanes], taps, load_sem.at[1]),
        pltpu.make_async_copy(table, tab, load_sem.at[2]),
        pltpu.make_async_copy(signal, sig_v, load_sem.at[3]),
        pltpu.make_async_copy(signal.at[:, lanes], xbuf.at[own], load_sem.at[4]),
        pltpu.make_async_copy(gate.at[:, lanes], gbuf.at[z], load_sem.at[5]),
        pltpu.make_async_copy(cotangent.at[:, lanes], cbuf.at[z], load_sem.at[6]),
        pltpu.make_async_copy(skip.at[:, lanes], skip_v, load_sem.at[7]),
        pltpu.make_async_copy(gate, gate_v, load_sem.at[8]),
        pltpu.make_async_copy(cotangent, cot_v, load_sem.at[9]),
    ]
    for load in loads:
        load.start()

    for load in loads[3:]:
        load.wait()
    pl.semaphore_wait(barrier, len(partners))

    def along_z(source, target, ssem, rsem):
        copies = {}
        for k in (2, 1, 3):
            copies[k] = send(source.at[:, chunk(z + k)], target, ssem.at[k - 1], rsem.at[k - 1], at(x, z + k, y))
            copies[k].start()
        return copies

    def back_along_z(source, result, ssem, rsem):
        copies = {}
        for k in (2, 1, 3):
            copies[k] = send(
                source.at[lax.rem(z + k, Q)], result.at[:, lanes], ssem.at[k - 1], rsem.at[k - 1], at(x, z + k, y)
            )
            copies[k].start()
        return copies

    def transform(tbl, buf, start, count, result):
        def body(i, _):
            pair = buf[pl.ds(start + 2 * i, 2)]
            wide = jnp.concatenate([pair[0], pair[1]], axis=1)
            value = dot(tab[tbl], jnp.concatenate([wide, wide], axis=0))
            result[start + 2 * i] = value[:, :C]
            result[start + 2 * i + 1] = value[:, C:]
            return 0

        lax.fori_loop(0, count // 2, body, 0)

    def inverse(rows, values):
        high = values.astype(BF16)
        low = (values - high.astype(F32)).astype(BF16)
        vh, vl = tab[2, rows, :], tab[3, rows, :]
        return dot(vh, high) + dot(vh, low) + dot(vl, high)

    def tile(f):
        return pl.ds(pl.multiple_of(8 * f, 8), 8), pl.ds(pl.multiple_of(T + 8 * f, 8), 8)

    waits = []
    halves = (pl.ds(0, T // 2), pl.ds(T // 2, T // 2))
    steps = (1, 3)
    relays = []
    for h, k in enumerate(steps):
        copy = send(sig_v.at[halves[h], chunk(z + 2)], rbuf.at[h], zr_s.at[h], zr_r.at[h], at(x, z + k, y))
        copy.start()
        relays.append(copy)
    for k in steps:
        copy = send(sig_v.at[:, chunk(z + k)], xbuf.at[own], za_s.at[k - 1], za_r.at[k - 1], at(x, z + k, y))
        copy.start()
        waits.append(copy)
    waits += relays
    for k in steps:
        pl.semaphore_signal(inside_sem, inc=1, device_id=at(x, z + k, y), device_id_type=MESH)
    sent = []
    late_loads = []

    def arrivals(zsrc):
        for j in (1, 2, 3):
            ysrc = lax.rem(y + 4 - j, Q)
            slot = xbuf.at[8 + 4 * zsrc + ysrc]
            copy = send(slot, slot, yf_s.at[0, j - 1], yf_r.at[zsrc, j - 1], at(x, z, ysrc))
            pl.when((zsrc < 3) | (y > ysrc))(copy.wait_recv)

    for k in (0, 1, 3, 2):
        zsrc = lax.rem(z + 4 - k, Q)
        slot = xbuf.at[8 + 4 * zsrc + y]
        if k == 2:
            for h in range(2):
                half = slot.at[halves[h]]
                send(half, half, zf_s.at[h], zf_r.at[h], at(x, z + 2, y)).wait_recv()
        elif k:
            send(slot, slot, za_s.at[k - 1], za_r.at[k - 1], at(x, z + k, y)).wait_recv()
        side = jnp.where(zsrc == 3, 1, 0)
        ways = [("y", j) for j in (2, 1, 3)]
        halo = [("x", j) for j in (2, 1, 3, 0)]
        for way, j in halo + ways if k == 2 else ways + halo:
            yp = lax.rem(y + j, Q)
            if way == "y":
                needed = (zsrc < 3) | (yp > y)
                copy = send(slot, slot, yf_s.at[k, j - 1], yf_r.at[zsrc, j - 1], at(x, z, yp))
            else:
                needed = (zsrc == 3) | ((zsrc == 2) & (yp < y))
                copy = send(slot, xbuf.at[4 * side + y], xh_s.at[k, j], xh_r.at[side, j], at(x + 1, z, yp))
            pl.when(needed)(copy.start)
            sent.append((needed, copy))
        if k == 0:
            for h, step in enumerate(steps):
                relays[h].wait_recv()
                half = xbuf.at[8 + 4 * lax.rem(z + 4 - step, Q) + y].at[halves[h]]
                copy = send(rbuf.at[h], half, zf_s.at[h], zf_r.at[h], at(x, z + step, y))
                copy.start()
                waits.append(copy)
        if k == 1:
            pl.semaphore_wait(inside_sem, 2)
            g_copies = along_z(gate_v, gbuf.at[z], ga_s, ga_r)
            c_copies = along_z(cot_v, cbuf.at[z], ca_s, ca_r)
            waits += list(g_copies.values()) + list(c_copies.values())
        if k == 3:
            loads[0].wait()
            early = []
            for zp in range(Q):
                block = 16 * x + 4 * zp + y
                begin, first, last = jnp.int32(0), jnp.int32(0), jnp.int32(0)
                for k in range(docs.shape[0]):
                    end = begin + docs_v[k]
                    inside = (begin <= block) & (block < end)
                    first = jnp.where(inside, begin, first)
                    last = jnp.where(inside, end, last)
                    begin = end
                early.append([jnp.where(block - d >= first, 1.0, 0.0).astype(F32) for d in range(LAGS)])
                for d in range(LAGS):
                    late_m[zp, d] = jnp.where(block + d < last, 1.0, 0.0).astype(F32)

            row0 = lax.broadcasted_iota(jnp.int32, (T, C), 0) == 0
            loads[1].wait()
            loads[2].wait()
            for d in range(LAGS):
                tap = taps[d * T : (d + 1) * T, :]
                value = dot(tab[1], jnp.concatenate([tap, tap], axis=0))
                if d > 0:
                    before = taps[(d - 1) * T : d * T, :]
                    value += dot(tab[0], jnp.concatenate([before, before], axis=0))
                real, imag = value[:T], value[T:]
                kr[d] = real
                ki[d] = jnp.where(row0, 0.0, imag)
                kn[d] = jnp.where(row0, imag, real)
            for step in (0, 1, 3):
                earlier = lax.rem(z + 4 - step, Q)
                arrivals(earlier)
                transform(0, xbuf, 8 + 4 * earlier, 4, spec)
    arrivals(zsrc)
    transform(0, xbuf, 8 + 4 * zsrc, 4, spec)
    for side in (0, 1):
        for j in range(Q):
            ysrc = lax.rem(y + 4 - j, Q)
            slot = xbuf.at[4 * side + ysrc]
            copy = send(slot, slot, xh_s.at[0, j], xh_r.at[side, j], at(x + 3, z, ysrc))
            if side:
                copy.wait_recv()
            else:
                pl.when(y < ysrc)(copy.wait_recv)
    transform(0, xbuf, 0, 8, spec)

    def forward_tile(f, _):
        re, im = tile(f)
        for zp in range(Q):
            acc_r = jnp.zeros((8, C), F32)
            acc_i = jnp.zeros((8, C), F32)
            for d in range(LAGS):
                r = 8 + 4 * zp + y - d
                live = early[zp][d]
                s_r, s_i = spec[r, re, :] * live, spec[r, im, :] * live
                acc_r += kr[d, re, :] * s_r - ki[d, re, :] * s_i
                acc_i += kn[d, re, :] * s_i + ki[d, re, :] * s_r
            prod[re, zp * C : (zp + 1) * C] = acc_r
            prod[im, zp * C : (zp + 1) * C] = acc_i
        return 0

    lax.fori_loop(0, T // 8, forward_tile, 0)
    conv = inverse(slice(T, 2 * T), prod[...])

    ones = jnp.ones((2 * C, C), BF16)
    lane = lax.broadcasted_iota(jnp.int32, (T, C), 1)
    sums = jnp.zeros((T, C), F32)
    for zp in range(Q):
        zval[zp] = conv[:, zp * C : (zp + 1) * C]
    for k in (0, 1, 3, 2):
        zp = lax.rem(z + Q - k, Q)
        if k:
            g_copies[k].wait_recv()
            c_copies[k].wait_recv()
        mixed = zval[zp] + skip_v[...] * xbuf[8 + 4 * zp + y].astype(F32)
        zval[zp] = mixed
        z_s[zp, 0] = mixed.astype(BF16)
        z_s[zp, 1] = (mixed - mixed.astype(BF16).astype(F32)).astype(BF16)
        gated = gbuf[zp].astype(F32) * mixed
        for number, values in ((zp, gated * gated), (Q + zp, cbuf[zp].astype(F32) * gated)):
            high = values.astype(BF16)
            low = (values - high.astype(F32)).astype(BF16)
            sums = jnp.where(lane == number, dot(jnp.concatenate([high, low], axis=1), ones), sums)
    own_r[...] = sums.T[:8]
    n_copies = []
    for i, (step, other) in enumerate(near):
        dst = far_r.at[i] if i < 2 else near_r.at[i - 2]
        copy = send(own_r, dst, n_ss.at[i], n_rs.at[i], ring(step, other))
        copy.start()
        n_copies.append(copy)
    for copy in n_copies[2:]:
        copy.wait_recv()
    total = own_r[...]
    for i in range(9):
        total += near_r[i]
    wide_s[...] = total
    w_copies = []
    for i, step in enumerate(wide):
        copy = send(wide_s, wide_r.at[i], w_ss.at[i], w_rs.at[i], ring(step, 0))
        copy.start()
        w_copies.append(copy)
    zb_copies = []
    for k in (2, 1, 3):
        copy = send(z_s.at[lax.rem(z + k, Q)], z_r.at[z], zb_s.at[k - 1], zb_r.at[k - 1], at(x, z + k, y))
        copy.start()
        zb_copies.append(copy)
    for copy in n_copies[:2] + w_copies:
        copy.wait_recv()
    waits += n_copies + w_copies
    mean = (total + (wide_r[0] + wide_r[1]) + (far_r[0] + far_r[1])) / (Q * C * 8)
    inv_rows = lax.rsqrt(mean[0:4] + EPSILON)
    fac_rows = mean[4:8] * inv_rows * inv_rows * inv_rows
    factors = jnp.concatenate([inv_rows, fac_rows], axis=0).T

    for zp in range(Q):
        inv = jnp.broadcast_to(factors[:, zp : zp + 1], (T, C))
        fac = jnp.broadcast_to(factors[:, 4 + zp : 5 + zp], (T, C))
        inv_b[zp] = inv
        fac_b[zp] = fac
        gate_f = gbuf[zp].astype(F32)
        dgated = cbuf[zp].astype(F32) * inv - gate_f * zval[zp] * fac
        dbuf[zp, y] = (dgated * gate_f).astype(BF16)

    def by_z(*values):
        result = jnp.int32(values[0])
        for number in range(1, Q):
            result = jnp.where(z == number, values[number], result)
        return result

    quads = [by_z(*row) for row in ((2, 3, 0, 1), (3, 4, 1, 2), (4, 5, 2, 3), (1, 2, 3, 0), (5, 0, 4, 4), (0, 1, 5, 5))]
    order = [by_z(*row) for row in ((2, 3, 0, 1), (1, 2, 1, 0), (3, 0, 3, 2), (0, 1, 2, 3))]

    def quad_copies(quad, way):
        result = []
        for j in (2, 1, 3, 0):
            other = lax.rem(y + Q + way * j, Q)
            source, target = (y, other) if way == 1 else (other, y)
            if j:
                own_quad = lax.rem(quad, Q)
                slot = dbuf.at[own_quad, source]
                copy = send(slot, slot, df_s.at[own_quad, j - 1], df_r.at[own_quad, j - 1], at(x, z, other))
                result.append(((quad < Q) & ((quad > 0) | (source > target)), copy))
            side = lax.rem(quad, 2)
            copy = send(
                dbuf.at[side, source], dbuf.at[4 + side, source], dh_s.at[side, j], dh_r.at[side, j],
                at(x + (3 if way == 1 else 1), z, other),
            )
            result.append(((quad == 4) | ((quad == 5) & (target > source)), copy))
        return result

    for quad in quads:
        for needed, copy in quad_copies(quad, 1):
            pl.when(needed)(copy.start)
            sent.append((needed, copy))

    own_d = jnp.concatenate([dbuf[zp, y] for zp in range(Q)], axis=1)
    own_spec = dot(tab[1], jnp.concatenate([own_d, own_d], axis=0))
    for zp in range(Q):
        dspec[4 * zp + y] = own_spec[:, zp * C : (zp + 1) * C]

    def filter_tile(f, _):
        re, im = tile(f)
        first = (lax.broadcasted_iota(jnp.int32, (8, C), 0) == 0) & (f == 0)
        sign = (1 - 2 * (lax.broadcasted_iota(jnp.int32, (8, C), 0) % 2)).astype(F32)
        mine = []
        for zp in range(Q):
            d_r, d_i = dspec[4 * zp + y, re, :], dspec[4 * zp + y, im, :]
            mine.append((d_r, jnp.where(first, 0.0, d_i), jnp.where(first, -d_i, d_r)))
        prior = None
        for d in range(LAGS):
            acc_r = jnp.zeros((8, C), F32)
            acc_i = jnp.zeros((8, C), F32)
            for zp in range(Q):
                r = 8 + 4 * zp + y - d
                live = early[zp][d]
                s_r, s_i = spec[r, re, :] * live, spec[r, im, :] * live
                d_r, d_i, d_n = mine[zp]
                acc_r += d_r * s_r + d_i * s_i
                acc_i += d_i * s_r - d_n * s_i
            if prior is not None:
                cols = slice((d - 1) * C, d * C)
                gprod[re, cols] = prior[0] * sign + acc_r
                gprod[im, cols] = prior[1] * sign + acc_i
            prior = (acc_r, acc_i)
        cols = slice((LAGS - 1) * C, LAGS * C)
        gprod[re, cols] = prior[0] * sign
        gprod[im, cols] = prior[1] * sign
        return 0

    lax.fori_loop(0, T // 8, filter_tile, 0)
    scale = float(64 * T) ** (-0.5)
    for half in range(Q):
        value = inverse(slice(0, T), gprod[:, 2 * half * C : 2 * (half + 1) * C]) * scale
        for odd in range(2):
            for i in range(8):
                piece = value[16 * i : 16 * i + 16, odd * C : (odd + 1) * C].astype(BF16)
                gf_s[half, i % 4, 2 * odd + i // 4] = piece
    gx_copies = []
    around = [(i, k) for i in (2, 1, 3, 0) for k in (2, 1, 3, 0) if i or k]
    for n, (i, k) in enumerate(around):
        copy = send(
            gf_s.at[lax.rem(x + i, Q), lax.rem(y + k, Q)], gf_r.at[n], gx_ss.at[n], gx_rs.at[n], at(x + i, z, y + k)
        )
        copy.start()
        gx_copies.append(copy)
    waits += gx_copies

    def arrive(quad):
        for needed, copy in quad_copies(quad, -1):
            pl.when(needed)(copy.wait_recv)
        blocks = jnp.concatenate([dbuf[quad, k] for k in range(Q)], axis=1)
        value = dot(tab[1], jnp.concatenate([blocks, blocks], axis=0))
        for k in range(Q):
            dspec[4 * quad + k] = value[:, k * C : (k + 1) * C]

    def signal_gradient(zp):
        def backward_tile(f, _):
            re, im = tile(f)
            acc_r = jnp.zeros((8, C), F32)
            acc_i = jnp.zeros((8, C), F32)
            for d in range(LAGS):
                r = 4 * zp + y + d
                live = late_m[zp, d]
                s_r, s_i = dspec[r, re, :] * live, dspec[r, im, :] * live
                acc_r += kr[d, re, :] * s_r + ki[d, re, :] * s_i
                acc_i += kn[d, re, :] * s_i - ki[d, re, :] * s_r
            prod[re, :C] = acc_r
            prod[im, :C] = acc_i
            return 0

        lax.fori_loop(0, T // 8, backward_tile, 0)
        conv = inverse(slice(0, T), prod[:, :C])
        gsig_s[zp] = (conv + skip_v[...] * dbuf[zp, y].astype(F32)).astype(BF16)

    s_copies = []

    def give(number):
        zp = order[number]
        step = lax.rem(zp + Q - z, Q) - 1
        signal_gradient(zp)
        copy = send(gsig_s.at[zp], gsig.at[:, lanes], sb_s.at[step], sb_r.at[step], at(x, zp, y))
        copy.start()
        s_copies.append(copy)

    for quad in quads[:3]:
        arrive(quad)
    give(0)
    arrive(quads[3])
    give(1)

    arrive(quads[4])
    arrive(quads[5])
    give(2)

    for copy in gx_copies:
        copy.wait_recv()
    total = gf_s[x, y].astype(F32)
    for n in range(len(around)):
        total += gf_r[n].astype(F32)
    gz_s[...] = total
    gz_copies = back_along_z(gz_s, gfilt, gz_ss, gz_rs)
    signal_gradient(z)

    z_r[z] = z_s[z]
    for copy in zb_copies:
        copy.wait()
    inv, fac = inv_b[z], fac_b[z]
    for j in range(Q):
        cols = slice(j * C, (j + 1) * C)
        mixed = z_r[j, 0].astype(F32) + z_r[j, 1].astype(F32)
        gated = gate_v[:, cols].astype(F32) * mixed
        dgated = cot_v[:, cols].astype(F32) * inv - gated * fac
        out_v[:, cols] = (gated * inv).astype(BF16)
        ggate_v[:, cols] = (dgated * mixed).astype(BF16)

    stores = [
        pltpu.make_async_copy(out_v, out, store_sem.at[0]),
        pltpu.make_async_copy(ggate_v, ggate, store_sem.at[1]),
        pltpu.make_async_copy(gsig_s.at[z], gsig.at[:, lanes], store_sem.at[2]),
        pltpu.make_async_copy(gz_s.at[z], gfilt.at[:, lanes], store_sem.at[3]),
    ]
    for copy in stores:
        copy.start()
    for copy in waits:
        copy.wait_send()
    for needed, copy in sent:
        if needed is None:
            copy.wait_send()
        else:
            pl.when(needed)(copy.wait_send)
    for copy in s_copies:
        copy.wait()
    for copy in list(gz_copies.values()) + stores:
        copy.wait()


def finish(a, b, c, d, e, f, g, h, sems):
    copies = [pltpu.make_async_copy(s, t, sems.at[i]) for i, (s, t) in enumerate(((a, e), (b, f), (c, g), (d, h)))]
    for copy in copies:
        copy.start()
    for copy in copies:
        copy.wait()


def on_device(signal, gate_input, filters, skip_weight, doc_lengths, grad_out):
    channels = signal.shape[1]
    vmem, hbm = pl.BlockSpec(memory_space=pltpu.VMEM), pl.BlockSpec(memory_space=pltpu.HBM)
    dma = lambda *shape: pltpu.SemaphoreType.DMA(shape)
    block = (T, channels)
    three = [dma(3)] * 2
    scratch = [
        pltpu.SMEM(doc_lengths.shape, jnp.int32), pltpu.SMEM((Q, LAGS), F32),
        pltpu.VMEM((1, C), F32),
        pltpu.VMEM(block, BF16), pltpu.VMEM(block, BF16), pltpu.VMEM(block, BF16),
        pltpu.VMEM((LAGS * T, C), BF16), pltpu.VMEM((4, 2 * T, 2 * T), BF16),
        pltpu.VMEM((24, T, C), BF16), pltpu.VMEM((Q, T, C), BF16), pltpu.VMEM((Q, T, C), BF16),
        pltpu.VMEM((6, Q, T, C), BF16), pltpu.VMEM((2, T // 2, C), BF16),
        pltpu.VMEM((24, 2 * T, C), F32), pltpu.VMEM((24, 2 * T, C), F32),
        pltpu.VMEM((LAGS, T, C), F32), pltpu.VMEM((LAGS, T, C), F32), pltpu.VMEM((LAGS, T, C), F32),
        pltpu.VMEM((2 * T, Q * C), F32), pltpu.VMEM((2 * T, LAGS * C), F32), pltpu.VMEM((Q, T, C), F32),
        pltpu.VMEM((Q, T, C), F32), pltpu.VMEM((Q, T, C), F32),
        pltpu.VMEM((Q, 2, T, C), BF16), pltpu.VMEM((Q, 2, T, C), BF16), pltpu.VMEM(block, BF16), pltpu.VMEM(block, BF16), pltpu.VMEM((Q, T, C), BF16),
        pltpu.VMEM((8, T), F32), pltpu.VMEM((9, 8, T), F32), pltpu.VMEM((2, 8, T), F32),
        pltpu.VMEM((8, T), F32), pltpu.VMEM((2, 8, T), F32),
        pltpu.VMEM((Q, Q, 4, 16, C), BF16), pltpu.VMEM((15, 4, 16, C), BF16), pltpu.VMEM((4, 16, C), F32),
        pltpu.SemaphoreType.REGULAR, dma(10), dma(4), *three, dma(2), dma(2), dma(2), dma(2), *three, *three, dma(4, 3), dma(4, 3), dma(4, 4), dma(2, 4), dma(11), dma(11), dma(2), dma(2),
        dma(4, 3), dma(4, 3), dma(2, 4), dma(2, 4), *three, *three, dma(15), dma(15), *three,
    ]
    shapes = (
        jax.ShapeDtypeStruct(block, BF16), jax.ShapeDtypeStruct(block, BF16),
        jax.ShapeDtypeStruct(block, BF16), jax.ShapeDtypeStruct((16, channels), F32),
    )
    results = pl.pallas_call(
        kernel,
        out_shape=shapes,
        in_specs=[hbm] * 7,
        out_specs=(hbm,) * 4,
        scratch_shapes=scratch,
        compiler_params=pltpu.CompilerParams(
            collective_id=0, has_side_effects=True, vmem_limit_bytes=63 << 20
        ),
        name="hyena",
    )(doc_lengths, skip_weight[None, :], signal, gate_input, filters, grad_out, jnp.asarray(tables()))
    return pl.pallas_call(
        finish,
        out_shape=shapes,
        in_specs=[vmem] * 4,
        out_specs=(hbm,) * 4,
        scratch_shapes=[dma(4)],
        name="finish",
    )(*results)


def solution(mesh):
    placed = (P("seq", "tp"), P("seq", "tp"), P(None, "tp"), P("tp"), P(), P("seq", "tp"))
    return jax.shard_map(
        on_device,
        mesh=mesh,
        in_specs=placed,
        out_specs=(P("seq", "tp"), P("seq", "tp"), P("seq", "tp"), P("seq", "tp")),
        check_vma=False,
    )
```

```python
import functools
import math

import jax
import jax.numpy as jnp
import numpy as np
from jax import lax
from jax.experimental import pallas as pl
from jax.experimental.pallas import tpu as pltpu
from jax.sharding import PartitionSpec as P

EPSILON = 1e-06
MESH = pl.DeviceIdType.MESH
T = 128
C = 128
Q = 4
LAGS = 8
REL = 20
F32 = jnp.float32
BF16 = jnp.bfloat16


def tables():
    freq = np.arange(T)[:, None]
    time = np.arange(2 * T)[None, :]
    phase = (freq * time % (2 * T)) * (2.0 * math.pi / (2 * T))
    real, imag = np.cos(phase), -np.sin(phase)
    imag[0] = 1 - 2 * (np.arange(2 * T) % 2)
    forward = np.concatenate([real, imag], axis=0)
    scale = np.full((2 * T, 1), 1.0 / T)
    scale[0] = scale[T] = 0.5 / T
    backward = (forward * scale).T

    def split(table):
        table = table.astype(np.float32)
        high = table.astype(jnp.bfloat16)
        low = (table - high.astype(np.float32)).astype(jnp.bfloat16)
        return high, low

    high, low = split(forward)
    first = np.concatenate([high[:, :T], low[:, :T]], axis=1)
    second = np.concatenate([high[:, T:], low[:, T:]], axis=1)
    back_high, back_low = split(backward)
    return np.stack([first, second, back_high, back_low])


def dot(a, b):
    return jnp.dot(a, b, preferred_element_type=F32)


def kernel(
    docs, skip, signal, gate, filters, cotangent, table,
    out, gsig, ggate, gfilt,
    docs_v, late_m, skip_v, sig_v, gate_v, cot_v, taps, tab, xbuf, gbuf, cbuf, dbuf, rbuf, spec, dspec, kr, ki, kn,
    prod, gprod, zval, inv_b, fac_b, z_s, z_r, out_v, ggate_v, gsig_s, own_r, near_r, far_r, wide_s, wide_r,
    gf_s, gf_r, gz_s,
    inside_sem, load_sem, store_sem, za_s, za_r, zr_s, zr_r, zf_s, zf_r, ga_s, ga_r, ca_s, ca_r, yf_s, yf_r, xh_s, xh_r, n_ss, n_rs, w_ss, w_rs,
    df_s, df_r, dh_s, dh_r, zb_s, zb_r, sb_s, sb_r, gx_ss, gx_rs, gz_ss, gz_rs,
):
    seq, tpi = lax.axis_index("seq"), lax.axis_index("tp")
    x, z, y = seq // 16, (seq // 4) % 4, seq % 4

    def at(xx, zz, yy):
        return (lax.rem(xx, Q) * 16 + lax.rem(zz, Q) * 4 + lax.rem(yy, Q), tpi)

    def send(src, dst, ssem, rsem, target):
        return pltpu.make_async_remote_copy(
            src_ref=src, dst_ref=dst, send_sem=ssem, recv_sem=rsem, device_id=target, device_id_type=MESH
        )

    barrier = pltpu.get_barrier_semaphore()
    partners = [at(x, z + k, y) for k in (1, 3)] + [at(x, z, y + k) for k in (1, 2, 3)]
    partners += [at(x + i, z, y + k) for i in (1, 3) for k in range(Q)] + [at(x + 2, z, y)]
    place, core = 4 * z + tpi // 2, lax.rem(tpi, 2)

    def ring(step, other):
        spot = lax.rem(place + step + 16, 16)
        return (16 * x + 4 * (spot // 4) + y, 2 * lax.rem(spot, 4) + lax.rem(core + other, 2))

    near = [(8, 0), (8, 1)] + [(step, other) for step in (2, -2, 1, -1) for other in (0, 1)] + [(0, 1)]
    wide = (5, -5)
    partners += [ring(step, other) for step, other in near[2:]]
    for partner in partners:
        pl.semaphore_signal(barrier, inc=1, device_id=partner, device_id_type=MESH)

    def chunk(k):
        return pl.ds(pl.multiple_of(lax.rem(k, Q) * C, C), C)

    lanes = chunk(z)
    own = 8 + 4 * z + y
    loads = [
        pltpu.make_async_copy(docs, docs_v, load_sem.at[0]),
        pltpu.make_async_copy(filters.at[:, lanes], taps, load_sem.at[1]),
        pltpu.make_async_copy(table, tab, load_sem.at[2]),
        pltpu.make_async_copy(signal, sig_v, load_sem.at[3]),
        pltpu.make_async_copy(signal.at[:, lanes], xbuf.at[own], load_sem.at[4]),
        pltpu.make_async_copy(gate.at[:, lanes], gbuf.at[z], load_sem.at[5]),
        pltpu.make_async_copy(cotangent.at[:, lanes], cbuf.at[z], load_sem.at[6]),
        pltpu.make_async_copy(skip.at[:, lanes], skip_v, load_sem.at[7]),
        pltpu.make_async_copy(gate, gate_v, load_sem.at[8]),
        pltpu.make_async_copy(cotangent, cot_v, load_sem.at[9]),
    ]
    for load in loads:
        load.start()

    for load in loads[3:]:
        load.wait()
    pl.semaphore_wait(barrier, len(partners))

    def along_z(source, target, ssem, rsem):
        copies = {}
        for k in (2, 1, 3):
            copies[k] = send(source.at[:, chunk(z + k)], target, ssem.at[k - 1], rsem.at[k - 1], at(x, z + k, y))
            copies[k].start()
        return copies

    def back_along_z(source, result, ssem, rsem):
        copies = {}
        for k in (2, 1, 3):
            copies[k] = send(
                source.at[lax.rem(z + k, Q)], result.at[:, lanes], ssem.at[k - 1], rsem.at[k - 1], at(x, z + k, y)
            )
            copies[k].start()
        return copies

    def transform(tbl, buf, start, count, result):
        def body(i, _):
            pair = buf[pl.ds(start + 2 * i, 2)]
            wide = jnp.concatenate([pair[0], pair[1]], axis=1)
            value = dot(tab[tbl], jnp.concatenate([wide, wide], axis=0))
            result[start + 2 * i] = value[:, :C]
            result[start + 2 * i + 1] = value[:, C:]
            return 0

        lax.fori_loop(0, count // 2, body, 0)

    def inverse(rows, values):
        high = values.astype(BF16)
        low = (values - high.astype(F32)).astype(BF16)
        vh, vl = tab[2, rows, :], tab[3, rows, :]
        return dot(vh, high) + dot(vh, low) + dot(vl, high)

    def tile(f):
        return pl.ds(pl.multiple_of(8 * f, 8), 8), pl.ds(pl.multiple_of(T + 8 * f, 8), 8)

    waits = []
    halves = (pl.ds(0, T // 2), pl.ds(T // 2, T // 2))
    steps = (1, 3)
    relays = []
    for h, k in enumerate(steps):
        copy = send(sig_v.at[halves[h], chunk(z + 2)], rbuf.at[h], zr_s.at[h], zr_r.at[h], at(x, z + k, y))
        copy.start()
        relays.append(copy)
    for k in steps:
        copy = send(sig_v.at[:, chunk(z + k)], xbuf.at[own], za_s.at[k - 1], za_r.at[k - 1], at(x, z + k, y))
        copy.start()
        waits.append(copy)
    waits += relays
    for k in steps:
        pl.semaphore_signal(inside_sem, inc=1, device_id=at(x, z + k, y), device_id_type=MESH)
    sent = []
    late_loads = []

    def arrivals(zsrc):
        for j in (1, 2, 3):
            ysrc = lax.rem(y + 4 - j, Q)
            slot = xbuf.at[8 + 4 * zsrc + ysrc]
            copy = send(slot, slot, yf_s.at[0, j - 1], yf_r.at[zsrc, j - 1], at(x, z, ysrc))
            pl.when((zsrc < 3) | (y > ysrc))(copy.wait_recv)

    for k in (0, 1, 3, 2):
        zsrc = lax.rem(z + 4 - k, Q)
        slot = xbuf.at[8 + 4 * zsrc + y]
        if k == 2:
            for h in range(2):
                half = slot.at[halves[h]]
                send(half, half, zf_s.at[h], zf_r.at[h], at(x, z + 2, y)).wait_recv()
        elif k:
            send(slot, slot, za_s.at[k - 1], za_r.at[k - 1], at(x, z + k, y)).wait_recv()
        side = jnp.where(zsrc == 3, 1, 0)
        ways = [("y", j) for j in (2, 1, 3)]
        halo = [("x", j) for j in (2, 1, 3, 0)]
        for way, j in halo + ways if k == 2 else ways + halo:
            yp = lax.rem(y + j, Q)
            if way == "y":
                needed = (zsrc < 3) | (yp > y)
                copy = send(slot, slot, yf_s.at[k, j - 1], yf_r.at[zsrc, j - 1], at(x, z, yp))
            else:
                needed = (zsrc == 3) | ((zsrc == 2) & (yp < y))
                copy = send(slot, xbuf.at[4 * side + y], xh_s.at[k, j], xh_r.at[side, j], at(x + 1, z, yp))
            pl.when(needed)(copy.start)
            sent.append((needed, copy))
        if k == 0:
            for h, step in enumerate(steps):
                relays[h].wait_recv()
                half = xbuf.at[8 + 4 * lax.rem(z + 4 - step, Q) + y].at[halves[h]]
                copy = send(rbuf.at[h], half, zf_s.at[h], zf_r.at[h], at(x, z + step, y))
                copy.start()
                waits.append(copy)
        if k == 1:
            pl.semaphore_wait(inside_sem, 2)
            g_copies = along_z(gate_v, gbuf.at[z], ga_s, ga_r)
            c_copies = along_z(cot_v, cbuf.at[z], ca_s, ca_r)
            waits += list(g_copies.values()) + list(c_copies.values())
        if k == 3:
            loads[0].wait()
            early = []
            for zp in range(Q):
                block = 16 * x + 4 * zp + y
                begin, first, last = jnp.int32(0), jnp.int32(0), jnp.int32(0)
                for k in range(docs.shape[0]):
                    end = begin + docs_v[k]
                    inside = (begin <= block) & (block < end)
                    first = jnp.where(inside, begin, first)
                    last = jnp.where(inside, end, last)
                    begin = end
                early.append([jnp.where(block - d >= first, 1.0, 0.0).astype(F32) for d in range(LAGS)])
                for d in range(LAGS):
                    late_m[zp, d] = jnp.where(block + d < last, 1.0, 0.0).astype(F32)

            row0 = lax.broadcasted_iota(jnp.int32, (T, C), 0) == 0
            loads[1].wait()
            loads[2].wait()
            for d in range(LAGS):
                tap = taps[d * T : (d + 1) * T, :]
                value = dot(tab[1], jnp.concatenate([tap, tap], axis=0))
                if d > 0:
                    before = taps[(d - 1) * T : d * T, :]
                    value += dot(tab[0], jnp.concatenate([before, before], axis=0))
                real, imag = value[:T], value[T:]
                kr[d] = real
                ki[d] = jnp.where(row0, 0.0, imag)
                kn[d] = jnp.where(row0, imag, real)
            for step in (0, 1, 3):
                earlier = lax.rem(z + 4 - step, Q)
                arrivals(earlier)
                transform(0, xbuf, 8 + 4 * earlier, 4, spec)
    arrivals(zsrc)
    transform(0, xbuf, 8 + 4 * zsrc, 4, spec)
    for side in (0, 1):
        for j in range(Q):
            ysrc = lax.rem(y + 4 - j, Q)
            slot = xbuf.at[4 * side + ysrc]
            copy = send(slot, slot, xh_s.at[0, j], xh_r.at[side, j], at(x + 3, z, ysrc))
            if side:
                copy.wait_recv()
            else:
                pl.when(y < ysrc)(copy.wait_recv)
    transform(0, xbuf, 0, 8, spec)

    def forward_tile(f, _):
        re, im = tile(f)
        for zp in range(Q):
            acc_r = jnp.zeros((8, C), F32)
            acc_i = jnp.zeros((8, C), F32)
            for d in range(LAGS):
                r = 8 + 4 * zp + y - d
                live = early[zp][d]
                s_r, s_i = spec[r, re, :] * live, spec[r, im, :] * live
                acc_r += kr[d, re, :] * s_r - ki[d, re, :] * s_i
                acc_i += kn[d, re, :] * s_i + ki[d, re, :] * s_r
            prod[re, zp * C : (zp + 1) * C] = acc_r
            prod[im, zp * C : (zp + 1) * C] = acc_i
        return 0

    lax.fori_loop(0, T // 8, forward_tile, 0)
    conv = inverse(slice(T, 2 * T), prod[...])

    ones = jnp.ones((2 * C, C), BF16)
    lane = lax.broadcasted_iota(jnp.int32, (T, C), 1)
    sums = jnp.zeros((T, C), F32)
    for zp in range(Q):
        zval[zp] = conv[:, zp * C : (zp + 1) * C]
    for k in (0, 1, 3, 2):
        zp = lax.rem(z + Q - k, Q)
        if k:
            g_copies[k].wait_recv()
            c_copies[k].wait_recv()
        mixed = zval[zp] + skip_v[...] * xbuf[8 + 4 * zp + y].astype(F32)
        zval[zp] = mixed
        z_s[zp, 0] = mixed.astype(BF16)
        z_s[zp, 1] = (mixed - mixed.astype(BF16).astype(F32)).astype(BF16)
        gated = gbuf[zp].astype(F32) * mixed
        for number, values in ((zp, gated * gated), (Q + zp, cbuf[zp].astype(F32) * gated)):
            high = values.astype(BF16)
            low = (values - high.astype(F32)).astype(BF16)
            sums = jnp.where(lane == number, dot(jnp.concatenate([high, low], axis=1), ones), sums)
    own_r[...] = sums.T[:8]
    n_copies = []
    for i, (step, other) in enumerate(near):
        dst = far_r.at[i] if i < 2 else near_r.at[i - 2]
        copy = send(own_r, dst, n_ss.at[i], n_rs.at[i], ring(step, other))
        copy.start()
        n_copies.append(copy)
    for copy in n_copies[2:]:
        copy.wait_recv()
    total = own_r[...]
    for i in range(9):
        total += near_r[i]
    wide_s[...] = total
    w_copies = []
    for i, step in enumerate(wide):
        copy = send(wide_s, wide_r.at[i], w_ss.at[i], w_rs.at[i], ring(step, 0))
        copy.start()
        w_copies.append(copy)
    zb_copies = []
    for k in (2, 1, 3):
        copy = send(z_s.at[lax.rem(z + k, Q)], z_r.at[z], zb_s.at[k - 1], zb_r.at[k - 1], at(x, z + k, y))
        copy.start()
        zb_copies.append(copy)
    for copy in n_copies[:2] + w_copies:
        copy.wait_recv()
    waits += n_copies + w_copies
    mean = (total + (wide_r[0] + wide_r[1]) + (far_r[0] + far_r[1])) / (Q * C * 8)
    inv_rows = lax.rsqrt(mean[0:4] + EPSILON)
    fac_rows = mean[4:8] * inv_rows * inv_rows * inv_rows
    factors = jnp.concatenate([inv_rows, fac_rows], axis=0).T

    for zp in range(Q):
        inv = jnp.broadcast_to(factors[:, zp : zp + 1], (T, C))
        fac = jnp.broadcast_to(factors[:, 4 + zp : 5 + zp], (T, C))
        inv_b[zp] = inv
        fac_b[zp] = fac
        gate_f = gbuf[zp].astype(F32)
        dgated = cbuf[zp].astype(F32) * inv - gate_f * zval[zp] * fac
        dbuf[zp, y] = (dgated * gate_f).astype(BF16)

    def by_z(*values):
        result = jnp.int32(values[0])
        for number in range(1, Q):
            result = jnp.where(z == number, values[number], result)
        return result

    quads = [by_z(*row) for row in ((2, 3, 0, 1), (3, 4, 1, 2), (4, 5, 2, 3), (1, 2, 3, 0), (5, 0, 4, 4), (0, 1, 5, 5))]
    order = [by_z(*row) for row in ((2, 3, 0, 1), (1, 2, 1, 0), (3, 0, 3, 2), (0, 1, 2, 3))]

    def quad_copies(quad, way):
        result = []
        for j in (2, 1, 3, 0):
            other = lax.rem(y + Q + way * j, Q)
            source, target = (y, other) if way == 1 else (other, y)
            if j:
                own_quad = lax.rem(quad, Q)
                slot = dbuf.at[own_quad, source]
                copy = send(slot, slot, df_s.at[own_quad, j - 1], df_r.at[own_quad, j - 1], at(x, z, other))
                result.append(((quad < Q) & ((quad > 0) | (source > target)), copy))
            side = lax.rem(quad, 2)
            copy = send(
                dbuf.at[side, source], dbuf.at[4 + side, source], dh_s.at[side, j], dh_r.at[side, j],
                at(x + (3 if way == 1 else 1), z, other),
            )
            result.append(((quad == 4) | ((quad == 5) & (target > source)), copy))
        return result

    for quad in quads:
        for needed, copy in quad_copies(quad, 1):
            pl.when(needed)(copy.start)
            sent.append((needed, copy))

    own_d = jnp.concatenate([dbuf[zp, y] for zp in range(Q)], axis=1)
    own_spec = dot(tab[1], jnp.concatenate([own_d, own_d], axis=0))
    for zp in range(Q):
        dspec[4 * zp + y] = own_spec[:, zp * C : (zp + 1) * C]

    def filter_tile(f, _):
        re, im = tile(f)
        first = (lax.broadcasted_iota(jnp.int32, (8, C), 0) == 0) & (f == 0)
        sign = (1 - 2 * (lax.broadcasted_iota(jnp.int32, (8, C), 0) % 2)).astype(F32)
        mine = []
        for zp in range(Q):
            d_r, d_i = dspec[4 * zp + y, re, :], dspec[4 * zp + y, im, :]
            mine.append((d_r, jnp.where(first, 0.0, d_i), jnp.where(first, -d_i, d_r)))
        prior = None
        for d in range(LAGS):
            acc_r = jnp.zeros((8, C), F32)
            acc_i = jnp.zeros((8, C), F32)
            for zp in range(Q):
                r = 8 + 4 * zp + y - d
                live = early[zp][d]
                s_r, s_i = spec[r, re, :] * live, spec[r, im, :] * live
                d_r, d_i, d_n = mine[zp]
                acc_r += d_r * s_r + d_i * s_i
                acc_i += d_i * s_r - d_n * s_i
            if prior is not None:
                cols = slice((d - 1) * C, d * C)
                gprod[re, cols] = prior[0] * sign + acc_r
                gprod[im, cols] = prior[1] * sign + acc_i
            prior = (acc_r, acc_i)
        cols = slice((LAGS - 1) * C, LAGS * C)
        gprod[re, cols] = prior[0] * sign
        gprod[im, cols] = prior[1] * sign
        return 0

    lax.fori_loop(0, T // 8, filter_tile, 0)
    scale = float(64 * T) ** (-0.5)
    for half in range(Q):
        value = inverse(slice(0, T), gprod[:, 2 * half * C : 2 * (half + 1) * C]) * scale
        for odd in range(2):
            for i in range(8):
                piece = value[16 * i : 16 * i + 16, odd * C : (odd + 1) * C].astype(BF16)
                gf_s[half, i % 4, 2 * odd + i // 4] = piece
    gx_copies = []
    around = [(i, k) for i in (2, 1, 3, 0) for k in (2, 1, 3, 0) if i or k]
    for n, (i, k) in enumerate(around):
        copy = send(
            gf_s.at[lax.rem(x + i, Q), lax.rem(y + k, Q)], gf_r.at[n], gx_ss.at[n], gx_rs.at[n], at(x + i, z, y + k)
        )
        copy.start()
        gx_copies.append(copy)
    waits += gx_copies

    def arrive(quad):
        for needed, copy in quad_copies(quad, -1):
            pl.when(needed)(copy.wait_recv)
        blocks = jnp.concatenate([dbuf[quad, k] for k in range(Q)], axis=1)
        value = dot(tab[1], jnp.concatenate([blocks, blocks], axis=0))
        for k in range(Q):
            dspec[4 * quad + k] = value[:, k * C : (k + 1) * C]

    def signal_gradient(zp):
        def backward_tile(f, _):
            re, im = tile(f)
            acc_r = jnp.zeros((8, C), F32)
            acc_i = jnp.zeros((8, C), F32)
            for d in range(LAGS):
                r = 4 * zp + y + d
                live = late_m[zp, d]
                s_r, s_i = dspec[r, re, :] * live, dspec[r, im, :] * live
                acc_r += kr[d, re, :] * s_r + ki[d, re, :] * s_i
                acc_i += kn[d, re, :] * s_i - ki[d, re, :] * s_r
            prod[re, :C] = acc_r
            prod[im, :C] = acc_i
            return 0

        lax.fori_loop(0, T // 8, backward_tile, 0)
        conv = inverse(slice(0, T), prod[:, :C])
        gsig_s[zp] = (conv + skip_v[...] * dbuf[zp, y].astype(F32)).astype(BF16)

    s_copies = []

    def give(number):
        zp = order[number]
        step = lax.rem(zp + Q - z, Q) - 1
        signal_gradient(zp)
        copy = send(gsig_s.at[zp], gsig.at[:, lanes], sb_s.at[step], sb_r.at[step], at(x, zp, y))
        copy.start()
        s_copies.append(copy)

    for quad in quads[:3]:
        arrive(quad)
    give(0)
    arrive(quads[3])
    give(1)

    arrive(quads[4])
    arrive(quads[5])
    for copy in gx_copies:
        copy.wait_recv()
    total = gf_s[x, y].astype(F32)
    for n in range(len(around)):
        total += gf_r[n].astype(F32)
    gz_s[...] = total
    gz_copies = back_along_z(gz_s, gfilt, gz_ss, gz_rs)
    give(2)

    signal_gradient(z)

    z_r[z] = z_s[z]
    for copy in zb_copies:
        copy.wait()
    inv, fac = inv_b[z], fac_b[z]
    for j in range(Q):
        cols = slice(j * C, (j + 1) * C)
        mixed = z_r[j, 0].astype(F32) + z_r[j, 1].astype(F32)
        gated = gate_v[:, cols].astype(F32) * mixed
        dgated = cot_v[:, cols].astype(F32) * inv - gated * fac
        out_v[:, cols] = (gated * inv).astype(BF16)
        ggate_v[:, cols] = (dgated * mixed).astype(BF16)

    stores = [
        pltpu.make_async_copy(out_v, out, store_sem.at[0]),
        pltpu.make_async_copy(ggate_v, ggate, store_sem.at[1]),
        pltpu.make_async_copy(gsig_s.at[z], gsig.at[:, lanes], store_sem.at[2]),
        pltpu.make_async_copy(gz_s.at[z], gfilt.at[:, lanes], store_sem.at[3]),
    ]
    for copy in stores:
        copy.start()
    for copy in waits:
        copy.wait_send()
    for needed, copy in sent:
        if needed is None:
            copy.wait_send()
        else:
            pl.when(needed)(copy.wait_send)
    for copy in s_copies:
        copy.wait()
    for copy in list(gz_copies.values()) + stores:
        copy.wait()


def finish(a, b, c, d, e, f, g, h, sems):
    copies = [pltpu.make_async_copy(s, t, sems.at[i]) for i, (s, t) in enumerate(((a, e), (b, f), (c, g), (d, h)))]
    for copy in copies:
        copy.start()
    for copy in copies:
        copy.wait()


def on_device(signal, gate_input, filters, skip_weight, doc_lengths, grad_out):
    channels = signal.shape[1]
    vmem, hbm = pl.BlockSpec(memory_space=pltpu.VMEM), pl.BlockSpec(memory_space=pltpu.HBM)
    dma = lambda *shape: pltpu.SemaphoreType.DMA(shape)
    block = (T, channels)
    three = [dma(3)] * 2
    scratch = [
        pltpu.SMEM(doc_lengths.shape, jnp.int32), pltpu.SMEM((Q, LAGS), F32),
        pltpu.VMEM((1, C), F32),
        pltpu.VMEM(block, BF16), pltpu.VMEM(block, BF16), pltpu.VMEM(block, BF16),
        pltpu.VMEM((LAGS * T, C), BF16), pltpu.VMEM((4, 2 * T, 2 * T), BF16),
        pltpu.VMEM((24, T, C), BF16), pltpu.VMEM((Q, T, C), BF16), pltpu.VMEM((Q, T, C), BF16),
        pltpu.VMEM((6, Q, T, C), BF16), pltpu.VMEM((2, T // 2, C), BF16),
        pltpu.VMEM((24, 2 * T, C), F32), pltpu.VMEM((24, 2 * T, C), F32),
        pltpu.VMEM((LAGS, T, C), F32), pltpu.VMEM((LAGS, T, C), F32), pltpu.VMEM((LAGS, T, C), F32),
        pltpu.VMEM((2 * T, Q * C), F32), pltpu.VMEM((2 * T, LAGS * C), F32), pltpu.VMEM((Q, T, C), F32),
        pltpu.VMEM((Q, T, C), F32), pltpu.VMEM((Q, T, C), F32),
        pltpu.VMEM((Q, 2, T, C), BF16), pltpu.VMEM((Q, 2, T, C), BF16), pltpu.VMEM(block, BF16), pltpu.VMEM(block, BF16), pltpu.VMEM((Q, T, C), BF16),
        pltpu.VMEM((8, T), F32), pltpu.VMEM((9, 8, T), F32), pltpu.VMEM((2, 8, T), F32),
        pltpu.VMEM((8, T), F32), pltpu.VMEM((2, 8, T), F32),
        pltpu.VMEM((Q, Q, 4, 16, C), BF16), pltpu.VMEM((15, 4, 16, C), BF16), pltpu.VMEM((4, 16, C), F32),
        pltpu.SemaphoreType.REGULAR, dma(10), dma(4), *three, dma(2), dma(2), dma(2), dma(2), *three, *three, dma(4, 3), dma(4, 3), dma(4, 4), dma(2, 4), dma(11), dma(11), dma(2), dma(2),
        dma(4, 3), dma(4, 3), dma(2, 4), dma(2, 4), *three, *three, dma(15), dma(15), *three,
    ]
    shapes = (
        jax.ShapeDtypeStruct(block, BF16), jax.ShapeDtypeStruct(block, BF16),
        jax.ShapeDtypeStruct(block, BF16), jax.ShapeDtypeStruct((16, channels), F32),
    )
    results = pl.pallas_call(
        kernel,
        out_shape=shapes,
        in_specs=[hbm] * 7,
        out_specs=(hbm,) * 4,
        scratch_shapes=scratch,
        compiler_params=pltpu.CompilerParams(
            collective_id=0, has_side_effects=True, vmem_limit_bytes=63 << 20
        ),
        name="hyena",
    )(doc_lengths, skip_weight[None, :], signal, gate_input, filters, grad_out, jnp.asarray(tables()))
    return pl.pallas_call(
        finish,
        out_shape=shapes,
        in_specs=[vmem] * 4,
        out_specs=(hbm,) * 4,
        scratch_shapes=[dma(4)],
        name="finish",
    )(*results)


def solution(mesh):
    placed = (P("seq", "tp"), P("seq", "tp"), P(None, "tp"), P("tp"), P(), P("seq", "tp"))
    return jax.shard_map(
        on_device,
        mesh=mesh,
        in_specs=placed,
        out_specs=(P("seq", "tp"), P("seq", "tp"), P("seq", "tp"), P("seq", "tp")),
        check_vma=False,
    )
```
